256 devices in a mesh: src: 8 (over z_hi, y), tgt: 32 (over z_lo, x, core).
Axes of the slice: x: 4, y: 4, z: 8 (z_hi: 2, z_lo: 4; z = z_hi * 4 + z_lo), core: 2. Of those that a mesh axis runs over, the one named last changes fastest.
Arguments:
- source_points: bfloat16 [16384, 128], P(('src', 'tgt')), may hold values from -1 to 1
- target_points: bfloat16 [32768, 128], P(('tgt', 'src')), may hold values from -1 to 1
- source_mass: float32 [16384], P('src'), may hold values from 0.1 to 10
- target_mass: float32 [32768], P('tgt'), may hold values from 0.1 to 10
Outputs:
- source_potential: float32 [16384], P('src')
- target_potential: float32 [32768], P('tgt')
The draws below stay inside these ranges and needn't reach their ends.
All inputs are finite; a program needn't handle non-finite values.
Results may differ from the reference program's by a relative error of at most 0.0003.
Values may be sent and summed in bfloat16 or wider, within the bound.
A program may use at most 64 MiB of HBM per device.

```python
import math
import jax
import jax.numpy as jnp
from jax import lax

D = 128
ITERS = 3
NS = 16384
NT = 32768


def shared_targets(key):
    base = 0.25 * jax.random.normal(key, (NT, D), jnp.float32)
    return jnp.clip(base, -1.0, 1.0)


def draw_source_points(key, part):
    key = jax.random.fold_in(key, 11)
    values = jnp.clip(0.25 * jax.random.normal(key, (NS, D), jnp.float32), -1.0, 1.0)
    return values.astype(jnp.bfloat16)


def draw_target_points(key, part):
    targets = shared_targets(key)
    return targets.astype(jnp.bfloat16)


def level_of(key, dims, split, low, high):
    loudness, own = 1.0, jax.random.fold_in(key, 6)
    for axis_at, parts in split:
        steps = jnp.exp(jax.random.uniform(jax.random.fold_in(own, axis_at), (parts,), jnp.float32, low / len(split), high / len(split)))
        loudness = loudness * jnp.repeat(steps, dims[axis_at] // parts).reshape([-1 if axis == axis_at else 1 for axis in range(len(dims))])
    return loudness


def setup_inputs(seed: int = 0) -> dict:
    arg_keys = jax.random.split(jax.random.key(seed), 5)
    source_points = draw_source_points(jax.random.fold_in(arg_keys[4], 71), 0)
    target_points = draw_target_points(jax.random.fold_in(arg_keys[4], 71), 0)
    source_mass = jnp.clip(jnp.exp(math.log(10.0) - 4.6051702 * jax.random.uniform(arg_keys[2], (NS,), jnp.float32) ** level_of(arg_keys[2], (NS,), ((0, 8),), -0.2, 0.2)), 0.1, 10.0)
    target_mass = jnp.clip(jnp.exp(math.log(10.0) - 4.6051702 * jax.random.uniform(arg_keys[3], (NT,), jnp.float32) ** level_of(arg_keys[3], (NT,), ((0, 32),), -0.2, 0.2)), 0.1, 10.0)
    return {"source_points": source_points, "target_points": target_points, "source_mass": source_mass, "target_mass": target_mass}


EPS = 0.05


def half_norm(points):
    values = points.astype(jnp.float32)
    return 0.5 * jnp.sum(values * values, axis=1)


def update(rows, cols, col_pot, col_logm):
    count = rows.shape[0]
    block = math.gcd(512, count)
    col_half = half_norm(cols)
    shift = col_pot + EPS * col_logm
    blocks = rows.reshape(count // block, block, rows.shape[1])

    def one_block(chosen):
        cost = half_norm(chosen)[:, None] + col_half[None, :] - jnp.dot(chosen, cols.T, preferred_element_type=jnp.float32)
        scores = (shift[None, :] - cost) / EPS
        peak = jnp.max(scores, axis=1)
        total = jnp.sum(jnp.exp(scores - peak[:, None]), axis=1)
        return -EPS * (peak + jnp.log(total))

    return lax.map(one_block, blocks).reshape(count)


def reference(source_points, target_points, source_mass, target_mass):
    log_a = jnp.log(source_mass)
    log_b = jnp.log(target_mass)
    target_potential = jnp.zeros((target_points.shape[0],), jnp.float32)
    source_potential = jnp.zeros((source_points.shape[0],), jnp.float32)
    for step in range(ITERS):
        source_potential = update(source_points, target_points, target_potential, log_b)
        target_potential = update(target_points, source_points, source_potential, log_a)
    return source_potential, target_potential
```

```python
import math

import jax
import jax.numpy as jnp
from jax import lax
from jax.experimental import pallas as pl
from jax.experimental.pallas import tpu as pltpu
from jax.sharding import PartitionSpec as P

MESH = pl.DeviceIdType.MESH

ITERS = 3
EPS = 0.05
ALPHA = 1.0 / (EPS * math.log(2.0))
INV_LN2 = 1.0 / math.log(2.0)

TILES = 16
CHUNKS = 8
HALVES = 2


def log2(value):
    return jnp.log(value) * INV_LN2


def place(z, y, x, c):
    return {"src": (z // 4) * 4 + y, "tgt": (z % 4) * 8 + x * 2 + c}


def chunk_of(z):
    return (z % 4) * 2 + z // 4


def plane_peer(p, z, y, x, c):
    return place(z, (y + p // 8) % 4, (x + (p // 2) % 4) % 4, (c + p % 2) % 2)


def row_norm(points):
    values = points.astype(jnp.float32)
    square = values * values
    high = square.astype(jnp.bfloat16)
    low = (square - high.astype(jnp.float32)).astype(jnp.bfloat16)
    ones = jnp.ones((8, 128), jnp.bfloat16)
    dims = (((1,), (1,)), ((), ()))
    total = lax.dot_general(ones, high, dims, preferred_element_type=jnp.float32) + lax.dot_general(
        ones, low, dims, preferred_element_type=jnp.float32
    )
    return (0.5 * ALPHA) * total[0:1, :]


def to_column(row):
    return jnp.transpose(jnp.broadcast_to(row, (128, 128)))


def kernel(
    xs, ys, am, bm, f_out, g_out,
    X, Y, ST, CB, amv, bmv, aux_t, aux_s, r_rows, part_f, recv_f, part_g, recv_g, f_part, f_all, part_e, recv_e,
    local_sem, x_recv, fwd_recv, y_recv, at_recv, as_recv, send_sem,
    f_send, f_recv, g_send, g_recv, o_send, o_recv, e_send, e_recv,
):
    s = lax.axis_index("src")
    t = lax.axis_index("tgt")
    z = (s // 4) * 4 + t // 8
    y = s % 4
    x = (t // 2) % 4
    c = t % 2
    zl = z % 4
    tile = y * 4 + x
    q = chunk_of(z)
    line = lambda p: place((z + p) % 8, y, x, c)

    copies = [
        pltpu.make_async_copy(ys, Y.at[q], local_sem.at[0]),
        pltpu.make_async_copy(xs, X.at[tile, pl.ds(c * 64, 64)], local_sem.at[1]),
        pltpu.make_async_copy(bm, bmv, local_sem.at[2]),
        pltpu.make_async_copy(am, amv, local_sem.at[3]),
    ]
    for copy in copies:
        copy.start()

    barrier = pltpu.get_barrier_semaphore()

    def greet_line(p, carry):
        pl.semaphore_signal(barrier, inc=1, device_id=line(p), device_id_type=MESH)
        return carry

    def greet_plane(p, carry):
        pl.semaphore_signal(barrier, inc=1, device_id=plane_peer(p, z, y, x, c), device_id_type=MESH)
        return carry

    def greet_rest(p, carry):
        pl.semaphore_signal(
            barrier, inc=1, device_id=place((z + 1 + p % 7) % 8, (y + 1 + p // 7) % 4, x, c), device_id_type=MESH
        )
        return carry

    lax.fori_loop(0, 21, greet_rest, 0)
    lax.fori_loop(1, 8, greet_line, 0)
    lax.fori_loop(1, 32, greet_plane, 0)

    for copy in copies:
        copy.wait()
    norm = row_norm(Y[q])
    aux_t[q, 0:1, :] = log2(bmv[pl.ds(s, 1), :]) - norm
    aux_t[q, 1:2, :] = norm
    aux_s[tile] = log2(amv[pl.ds(t // 2, 1), :])

    pl.semaphore_wait(barrier, 7 + 31 + 21)

    def remote(src, dst, send, recv, device):
        pltpu.make_async_remote_copy(
            src_ref=src, dst_ref=dst, send_sem=send, recv_sem=recv, device_id=device, device_id_type=MESH
        ).start()

    def send_aux_t(p, carry):
        remote(aux_t.at[q], aux_t.at[q], send_sem.at[0], at_recv.at[0], line(p))
        return carry

    def send_y(k, carry):
        p = (4 + (k // 2 + k % 2) * (1 - 2 * (k % 2))) % 8
        remote(Y.at[q], Y.at[q], send_sem.at[1], y_recv.at[q], line(p))
        return carry

    own = (tile, pl.ds(c * 64, 64))

    def send_x(p, carry):
        device = plane_peer(p * 2, z, y, x, c)
        remote(X.at[own], X.at[own], send_sem.at[2], x_recv.at[tile], device)
        return carry

    def send_aux_s(p, carry):
        device = plane_peer(p * 2, z, y, x, c)
        remote(aux_s.at[tile], aux_s.at[tile], send_sem.at[3], as_recv.at[0], device)
        return carry

    sibling = place(z, y, x, 1 - c)
    lax.fori_loop(1, 8, send_aux_t, 0)
    lax.fori_loop(0, 7, send_y, 0)
    lax.fori_loop(1, 16, send_x, 0)
    lax.fori_loop(1, 16, send_aux_s, 0)
    remote(X.at[own], X.at[own], send_sem.at[4], fwd_recv.at[0], sibling)

    def forward(p, carry):
        there = ((y + p // 4) % 4) * 4 + (x + p % 4) % 4
        block = (there, pl.ds(c * 64, 64))
        pltpu.make_async_copy(X.at[block], X.at[block], x_recv.at[there]).wait()
        remote(X.at[block], X.at[block], send_sem.at[4], fwd_recv.at[0], sibling)
        return carry

    lax.fori_loop(1, 16, forward, 0)
    pltpu.make_async_copy(aux_t.at[pl.ds(0, 7)], aux_t.at[pl.ds(0, 7)], at_recv.at[0]).wait()
    pltpu.make_async_copy(aux_s.at[pl.ds(0, 15)], aux_s.at[pl.ds(0, 15)], as_recv.at[0]).wait()

    def columns(k, carry):
        CB[k] = to_column(aux_t[k, 0:1, :])
        return carry

    lax.fori_loop(0, CHUNKS, columns, 0)
    others = (pl.ds(0, TILES), pl.ds((1 - c) * 64, 64))
    pltpu.make_async_copy(X.at[others], X.at[others], fwd_recv.at[0]).wait()

    def scores_chunk(k, carry):
        p = ((k + 1) // 2) * (2 * (k % 2) - 1) + 8
        there = chunk_of((z + p) % 8)

        @pl.when(k > 0)
        def _():
            pltpu.make_async_copy(Y.at[there], Y.at[there], y_recv.at[there]).wait()

        chosen = Y[there]

        def scores_tile(m, carry):
            for u in range(4):
                ST[there, m * 4 + u] = ALPHA * lax.dot_general(
                    chosen, X[m * 4 + u], (((1,), (1,)), ((), ())), preferred_element_type=jnp.float32
                )
            return carry

        lax.fori_loop(0, TILES // 4, scores_tile, 0)
        return carry

    lax.fori_loop(0, CHUNKS, scores_chunk, 0)

    def source_tile(m):
        peak = None
        for k in range(CHUNKS):
            block = (ST[k, m] + CB[k]).reshape(16, 8, 128)
            here = jnp.max(block, axis=0)
            total_here = jnp.sum(jnp.exp2(block - here[None]), axis=0)
            if peak is None:
                peak, total = here, total_here
            else:
                top = jnp.maximum(peak, here)
                total = total * jnp.exp2(peak - top) + total_here * jnp.exp2(here - top)
                peak = top
        top = jnp.max(peak, axis=0, keepdims=True)
        return top + log2(jnp.sum(total * jnp.exp2(peak - top), axis=0, keepdims=True))

    def target_chunk(k, parts):
        def block(j, carry):
            rows = pl.ds(j * 8, 8)
            pieces = [ST[k, m, rows, :] + r_rows[m // 8, m % 8 : m % 8 + 1, :] for m in range(TILES)]
            peak = pieces[0]
            for piece in pieces[1:]:
                peak = jnp.maximum(peak, piece)
            total = jnp.exp2(pieces[0] - peak)
            for piece in pieces[1:]:
                total = total + jnp.exp2(piece - peak)
            parts[rows, :] = peak + log2(total)
            return carry

        lax.fori_loop(0, 16, block, 0, unroll=2)
        turned = jnp.transpose(parts[...])
        top = jnp.max(turned, axis=0, keepdims=True)
        return top + log2(jnp.sum(jnp.exp2(turned - top), axis=0, keepdims=True))

    def merge(parts):
        top = jnp.max(parts, axis=0)
        return top + log2(jnp.sum(jnp.exp2(parts - top[None]), axis=0))

    for step in range(ITERS):
        last = step == ITERS - 1
        for half in range(HALVES):

            def one_tile(m, carry):
                part_f[step, half, pl.ds(m, 1), :] = source_tile(half * 8 + m)
                return carry

            lax.fori_loop(0, 8, one_tile, 0)

            def send_f(p, carry):
                remote(
                    part_f.at[step, half], recv_f.at[step, half, p - 1], f_send.at[step, half], f_recv.at[step, half],
                    plane_peer(p, z, y, x, c),
                )
                return carry

            lax.fori_loop(1, 32, send_f, 0)
        for half in range(HALVES):
            arrived = recv_f.at[step, half]
            pltpu.make_async_copy(arrived, arrived, f_recv.at[step, half]).wait()
            total = merge(jnp.concatenate([recv_f[step, half], part_f[step, half][None]], axis=0))
            r_rows[half] = jnp.concatenate([aux_s[half * 8 + m] for m in range(8)], axis=0) - total
            if last:
                for m in range(8):
                    there = half * 8 + m
                    f_part[there // 4, there % 4 : there % 4 + 1, :] = row_norm(X[there]) - total[m : m + 1, :]
        if last:
            f_all[zl] = f_part[y]
            for p in range(1, 4):
                device = place((z // 4) * 4 + (zl + p) % 4, y, x, c)
                remote(f_part.at[y], f_all.at[zl], o_send.at[0], o_recv.at[0], device)

        if not last:

            def one_chunk(k, carry):
                part_g[step, k // 2, pl.ds(k % 2, 1), :] = target_chunk(k, part_e)
                return carry

            lax.fori_loop(0, CHUNKS, one_chunk, 0)

            def send_g(p, carry):
                remote(part_g.at[step], recv_g.at[step, p - 1], g_send.at[step], g_recv.at[step], line(p))
                return carry

            lax.fori_loop(1, 8, send_g, 0)
            arrived = recv_g.at[step]
            pltpu.make_async_copy(arrived, arrived, g_recv.at[step]).wait()
            total = merge(jnp.concatenate([recv_g[step], part_g[step][None]], axis=0))
            part_g[2] = total

            def columns_next(k, carry):
                row = pl.ds(k % 2, 1)
                CB[k] = to_column(aux_t[k, 0:1, :] + aux_t[k, 1:2, :] - part_g[2, k // 2, row, :])
                return carry

            lax.fori_loop(0, CHUNKS, columns_next, 0)
        else:

            def last_chunk(k, carry):
                part_g[step, k // 2, pl.ds(k % 2, 1), :] = target_chunk(k, part_e) - aux_t[k, 1:2, :]
                return carry

            lax.fori_loop(0, CHUNKS, last_chunk, 0)

            def send_e(p, carry):
                there = (z + p % 8) % 8
                remote(
                    part_g.at[step, there % 4], recv_e.at[y * 8 + z], e_send.at[0], e_recv.at[0],
                    place(there, (y + p // 8) % 4, x, c),
                )
                return carry

            lax.fori_loop(1, 32, send_e, 0)
            recv_e[y * 8 + z] = part_g[step, zl]
            others = recv_e.at[pl.ds(0, 31)]
            pltpu.make_async_copy(others, others, e_recv.at[0]).wait()
            for there in range(4):
                total = merge(recv_e[there * 8 : there * 8 + 8])
                for half in range(2):
                    g_out[half * 4 + there : half * 4 + there + 1, :] = -total[half : half + 1, :]

    arrived = f_all.at[pl.ds(0, 3)]
    pltpu.make_async_copy(arrived, arrived, o_recv.at[0]).wait()
    for there in range(4):
        f_out[there * 4 : there * 4 + 4, :] = f_all[there]

    def sent(ref, sem):
        pltpu.make_async_copy(ref, ref, sem).wait()

    sent(aux_t.at[pl.ds(0, 7)], send_sem.at[0])
    sent(Y.at[pl.ds(0, 7)], send_sem.at[1])
    sent(X.at[pl.ds(0, 15), pl.ds(0, 64)], send_sem.at[2])
    sent(aux_s.at[pl.ds(0, 15)], send_sem.at[3])
    sent(X.at[pl.ds(0, 16), pl.ds(0, 64)], send_sem.at[4])
    for step in range(ITERS):
        for half in range(HALVES):
            sent(recv_f.at[step, half], f_send.at[step, half])
        if step < ITERS - 1:
            sent(recv_g.at[step], g_send.at[step])
    sent(f_all.at[pl.ds(0, 3)], o_send.at[0])
    sent(recv_e.at[pl.ds(0, 31)], e_send.at[0])


def local(source_points, target_points, source_mass, target_mass):
    f32, bf16 = jnp.float32, jnp.bfloat16
    dma = pltpu.SemaphoreType.DMA
    f_scaled, g_scaled = pl.pallas_call(
        kernel,
        out_shape=(jax.ShapeDtypeStruct((16, 128), f32), jax.ShapeDtypeStruct((8, 128), f32)),
        in_specs=[pl.BlockSpec(memory_space=pl.ANY)] * 4,
        out_specs=[pl.BlockSpec(memory_space=pltpu.VMEM)] * 2,
        scratch_shapes=[
            pltpu.VMEM((TILES, 128, 128), bf16),
            pltpu.VMEM((CHUNKS, 128, 128), bf16),
            pltpu.VMEM((CHUNKS, TILES, 128, 128), f32),
            pltpu.VMEM((CHUNKS, 128, 128), f32),
            pltpu.VMEM((16, 128), f32),
            pltpu.VMEM((8, 128), f32),
            pltpu.VMEM((CHUNKS, 2, 128), f32),
            pltpu.VMEM((TILES, 1, 128), f32),
            pltpu.VMEM((2, 8, 128), f32),
            pltpu.VMEM((ITERS, HALVES, 8, 128), f32),
            pltpu.VMEM((ITERS, HALVES, 31, 8, 128), f32),
            pltpu.VMEM((ITERS, 4, 2, 128), f32),
            pltpu.VMEM((ITERS - 1, 7, 4, 2, 128), f32),
            pltpu.VMEM((4, 4, 128), f32),
            pltpu.VMEM((4, 4, 128), f32),
            pltpu.VMEM((128, 128), f32),
            pltpu.VMEM((32, 2, 128), f32),
            dma((4,)),
            dma((TILES,)),
            dma((1,)),
            dma((CHUNKS,)),
            dma((1,)),
            dma((1,)),
            dma((5,)),
            dma((ITERS, HALVES)),
            dma((ITERS, HALVES)),
            dma((ITERS,)),
            dma((ITERS,)),
            dma((1,)),
            dma((1,)),
            dma((1,)),
            dma((1,)),
        ],
        compiler_params=pltpu.CompilerParams(collective_id=0, has_side_effects=True, vmem_limit_bytes=40 * 2**20),
    )(source_points, target_points, source_mass.reshape(16, 128), target_mass.reshape(8, 128))
    return f_scaled.reshape(2048) * (1.0 / ALPHA), g_scaled.reshape(1024) * (1.0 / ALPHA)


def solution(mesh):
    placed = (P(("src", "tgt"), None), P(("tgt", "src"), None), P("src"), P("tgt"))
    return jax.shard_map(
        local, mesh=mesh, in_specs=placed, out_specs=(P("src"), P("tgt")), check_vma=False
    )
```

```python
import math

import jax
import jax.numpy as jnp
from jax import lax
from jax.experimental import pallas as pl
from jax.experimental.pallas import tpu as pltpu
from jax.sharding import PartitionSpec as P

MESH = pl.DeviceIdType.MESH

ITERS = 3
EPS = 0.05
ALPHA = 1.0 / (EPS * math.log(2.0))
INV_LN2 = 1.0 / math.log(2.0)

TILES = 16
CHUNKS = 8
LOW = -1e30
VMEM_LIMIT = 60 * 2**20


def log2(value):
    return jnp.log(value) * INV_LN2


def place(z, y, x, c):
    return {"src": (z // 4) * 4 + y, "tgt": (z % 4) * 8 + x * 2 + c}


def chunk_of(z):
    return (z % 4) * 2 + z // 4


def plane_peer(p, z, y, x, c):
    return place(z, (y + p // 8) % 4, (x + (p // 2) % 4) % 4, (c + p % 2) % 2)


def near_first(k):
    return ((k + 1) // 2 * (2 * (k % 2) - 1) + 8) % 8


def row_norm(points):
    values = points.astype(jnp.float32)
    square = values * values
    high = square.astype(jnp.bfloat16)
    low = (square - high.astype(jnp.float32)).astype(jnp.bfloat16)
    ones = jnp.ones((8, 128), jnp.bfloat16)
    dims = (((1,), (1,)), ((), ()))
    total = lax.dot_general(ones, high, dims, preferred_element_type=jnp.float32) + lax.dot_general(
        ones, low, dims, preferred_element_type=jnp.float32
    )
    return (0.5 * ALPHA) * total[0:1, :]


def to_column(row):
    return jnp.transpose(jnp.broadcast_to(row, (128, 128)))


def tree(op, values):
    values = list(values)
    while len(values) > 1:
        values = [op(*values[i : i + 2]) if i + 1 < len(values) else values[i] for i in range(0, len(values), 2)]
    return values[0]


def stats(pieces):
    peak = tree(jnp.maximum, pieces)
    return peak, tree(jnp.add, [jnp.exp2(piece - peak) for piece in pieces])


def join(first, second):
    peak = jnp.maximum(first[0], second[0])
    return peak, first[1] * jnp.exp2(first[0] - peak) + second[1] * jnp.exp2(second[0] - peak)


def merge(parts, own):
    top = jnp.maximum(jnp.max(parts, axis=0), own)
    return top + log2(jnp.sum(jnp.exp2(parts - top[None]), axis=0) + jnp.exp2(own - top))


def kernel(
    xs, ys, am, bm, f_out, g_out,
    X, Y, ST, CB, GM, GT, PM, PT, amv, bmv, aux_t, aux_s, logs_a, norm_x, r_rows,
    part_f, recv_f, part_g, recv_g, f_part, f_all, part_e, recv_e,
    local_sem, x_recv, fwd_recv, y_recv, at_recv, as_recv, send_sem,
    f_send, f_recv, g_send, g_recv, o_send, o_recv, e_send, e_recv,
):
    s = lax.axis_index("src")
    t = lax.axis_index("tgt")
    z = (s // 4) * 4 + t // 8
    y = s % 4
    x = (t // 2) % 4
    c = t % 2
    zl = z % 4
    tile = y * 4 + x
    q = chunk_of(z)
    line = lambda p: place((z + p) % 8, y, x, c)

    copies = [
        pltpu.make_async_copy(ys, Y.at[q], local_sem.at[0]),
        pltpu.make_async_copy(xs, X.at[tile, pl.ds(c * 64, 64)], local_sem.at[1]),
        pltpu.make_async_copy(bm, bmv, local_sem.at[2]),
        pltpu.make_async_copy(am, amv, local_sem.at[3]),
    ]
    for copy in copies:
        copy.start()

    barrier = pltpu.get_barrier_semaphore()

    def greet_line(p, carry):
        pl.semaphore_signal(barrier, inc=1, device_id=line(p), device_id_type=MESH)
        return carry

    def greet_plane(p, carry):
        pl.semaphore_signal(barrier, inc=1, device_id=plane_peer(p, z, y, x, c), device_id_type=MESH)
        return carry

    lax.fori_loop(1, 8, greet_line, 0)
    lax.fori_loop(1, 32, greet_plane, 0)

    for copy in copies:
        copy.wait()
    norm = row_norm(Y[q])
    aux_t[q, 0:1, :] = log2(bmv[pl.ds(s, 1), :]) - norm
    aux_t[q, 1:2, :] = norm
    aux_s[tile] = log2(amv[pl.ds(t // 2, 1), :])
    GM[...] = jnp.full((TILES, 8, 128), LOW, jnp.float32)
    GT[...] = jnp.zeros((TILES, 8, 128), jnp.float32)

    pl.semaphore_wait(barrier, 7 + 31)

    def remote(src, dst, send, recv, device):
        pltpu.make_async_remote_copy(
            src_ref=src, dst_ref=dst, send_sem=send, recv_sem=recv, device_id=device, device_id_type=MESH
        ).start()

    def arrived(ref, sem):
        pltpu.make_async_copy(ref, ref, sem).wait()

    def send_aux_t(p, carry):
        remote(aux_t.at[q], aux_t.at[q], send_sem.at[0], at_recv.at[0], line(p))
        return carry

    def send_y(k, carry):
        remote(Y.at[q], Y.at[q], send_sem.at[1], y_recv.at[q], line(near_first(7 - k)))
        return carry

    own = (tile, pl.ds(c * 64, 64))

    def send_x(p, carry):
        remote(X.at[own], X.at[own], send_sem.at[2], x_recv.at[tile], plane_peer(p * 2, z, y, x, c))
        return carry

    def send_aux_s(p, carry):
        remote(aux_s.at[tile], aux_s.at[tile], send_sem.at[3], as_recv.at[0], plane_peer(p * 2, z, y, x, c))
        return carry

    sibling = place(z, y, x, 1 - c)
    lax.fori_loop(1, 8, send_aux_t, 0)
    lax.fori_loop(0, 7, send_y, 0)
    lax.fori_loop(1, 16, send_x, 0)
    remote(X.at[own], X.at[own], send_sem.at[4], fwd_recv.at[tile], sibling)
    lax.fori_loop(1, 16, send_aux_s, 0)

    arrived(aux_t.at[pl.ds(0, 7)], at_recv.at[0])
    for k in range(CHUNKS):
        CB[k] = to_column(aux_t[k, 0:1, :])

    def row_of(n):
        return (y + (n + 1) // 2 * (2 * (n % 2) - 1) + 4) % 4

    def forward(n):
        for x_there in range(4):
            there = row_of(n) * 4 + x_there
            block = (there, pl.ds(c * 64, 64))

            @pl.when(there != tile)
            def _():
                arrived(X.at[block], x_recv.at[there])
                remote(X.at[block], X.at[block], send_sem.at[4], fwd_recv.at[there], sibling)

    def send_f(step, half):
        def to_peer(p, carry):
            remote(
                part_f.at[step, half], recv_f.at[step, half, p - 1], f_send.at[step, half], f_recv.at[step, half],
                plane_peer(p, z, y, x, c),
            )
            return carry

        lax.fori_loop(1, 32, to_peer, 0)

    def finish_sources(step, half):
        peaks = GM[pl.ds(half * 8, 8)]
        top = jnp.max(peaks, axis=1)
        total = jnp.sum(GT[pl.ds(half * 8, 8)] * jnp.exp2(peaks - top[:, None, :]), axis=1)
        part_f[step, half] = top + log2(total)
        send_f(step, half)

    forward(0)

    def scores(i, carry):
        pair = i // 4
        n = i % 4
        later = (pair + 3) // 4
        group = (later * n + (1 - later) * row_of(n)) % 4

        @pl.when(pair == 0)
        def _():
            @pl.when(n < 3)
            def _():
                forward(n + 1)

            for x_there in range(4):
                there = group * 4 + x_there
                arrived(X.at[there, pl.ds((1 - c) * 64, 64)], fwd_recv.at[there])

        chunks = [chunk_of((z + near_first(pair * 2 + u)) % 8) for u in range(2)]

        @pl.when(n == 0)
        def _():
            @pl.when(pair > 0)
            def _():
                arrived(Y.at[chunks[0]], y_recv.at[chunks[0]])

            arrived(Y.at[chunks[1]], y_recv.at[chunks[1]])

        rows = jnp.concatenate([Y[k] for k in chunks], axis=0)
        tiles = X[pl.ds(group * 4, 4)].reshape(512, 128)
        product = lax.dot_general(rows, tiles, (((1,), (1,)), ((), ())), preferred_element_type=jnp.float32)
        for m in range(4):
            found = []
            for u in range(2):
                pieces = []
                for j in range(16):
                    piece = ALPHA * product[(u * 16 + j) * 8 : (u * 16 + j + 1) * 8, m * 128 : (m + 1) * 128]
                    ST[chunks[u], group * 4 + m, j * 8 : j * 8 + 8, :] = piece
                    pieces.append(piece + CB[chunks[u], j * 8 : j * 8 + 8, :])
                found.append(stats(pieces))
            GM[group * 4 + m], GT[group * 4 + m] = join((GM[group * 4 + m], GT[group * 4 + m]), join(*found))

        @pl.when((pair == 3) & (n % 2 == 1))
        def _():
            finish_sources(0, n // 2)

        return carry

    lax.fori_loop(0, 16, scores, 0)

    arrived(aux_s.at[pl.ds(0, 15)], as_recv.at[0])
    for half in range(2):
        logs_a[half] = jnp.concatenate([aux_s[half * 8 + m] for m in range(8)], axis=0)

    def norms(m, carry):
        norm_x[m] = row_norm(X[m])
        return carry

    lax.fori_loop(0, TILES, norms, 0)

    def merged_f(step, half):
        arrived(recv_f.at[step, half], f_recv.at[step, half])
        total = merge(recv_f[step, half], part_f[step, half])
        r_rows[half] = logs_a[half] - total
        return total

    def target_pieces(k, j, half):
        return [
            ST[k, half * 8 + m, j * 8 : j * 8 + 8, :] + r_rows[half, m : m + 1, :] for m in range(8)
        ]

    def target_first():
        def chunk(k, carry):
            for j in range(16):
                rows = slice(j * 8, j * 8 + 8)
                PM[k, rows, :], PT[k, rows, :] = stats(target_pieces(k, j, 0))
            return carry

        lax.fori_loop(0, CHUNKS, chunk, 0)

    def target_second(half):
        def chunk(i, carry):
            k = half * 4 + i
            for j in range(16):
                rows = slice(j * 8, j * 8 + 8)
                PM[k, rows, :], PT[k, rows, :] = join((PM[k, rows, :], PT[k, rows, :]), stats(target_pieces(k, j, 1)))
            return carry

        lax.fori_loop(0, 4, chunk, 0)
        results = []
        for i in range(4):
            peak, total = jnp.transpose(PM[half * 4 + i]), jnp.transpose(PT[half * 4 + i])
            top = jnp.max(peak, axis=0, keepdims=True)
            results.append(top + log2(jnp.sum(total * jnp.exp2(peak - top), axis=0, keepdims=True)))
        return results

    def merged_g(step, half):
        arrived(recv_g.at[step, half], g_recv.at[step, half])
        total = merge(recv_g[step, half], part_g[step, half])
        for i in range(4):
            k = half * 4 + i
            CB[k] = to_column(aux_t[k, 0:1, :] + aux_t[k, 1:2, :] - total[i : i + 1, :])

    def source_tiles(first, half):
        for u in range(4):
            m = first + u
            for k in range(half * 4, half * 4 + 4):
                found = stats(
                    [ST[k, m, j * 8 : j * 8 + 8, :] + CB[k, j * 8 : j * 8 + 8, :] for j in range(16)]
                )
                state = found if k == half * 4 else join(state, found)
            if half == 1:
                state = join((GM[m], GT[m]), state)
            GM[m], GT[m] = state

    def iteration(step, carry):
        merged_f(step, 0)
        target_first()
        merged_f(step, 1)

        def target_half(half, carry):
            for i, row in enumerate(target_second(half)):
                part_g[step, half, i : i + 1, :] = row

            def send_g(p, carry):
                remote(part_g.at[step, half], recv_g.at[step, half, p - 1], g_send.at[step, half], g_recv.at[step, half], line(p))
                return carry

            return lax.fori_loop(1, 8, send_g, carry)

        lax.fori_loop(0, 2, target_half, 0)

        merged_g(step, 0)

        def first_tiles(i, carry):
            source_tiles(i * 4, 0)
            return carry

        lax.fori_loop(0, 4, first_tiles, 0)
        merged_g(step, 1)

        def source_half(half, carry):
            def more_tiles(i, carry):
                source_tiles(half * 8 + i * 4, 1)
                return carry

            lax.fori_loop(0, 2, more_tiles, 0)
            finish_sources(step + 1, half)
            return carry

        return lax.fori_loop(0, 2, source_half, carry)

    lax.fori_loop(0, ITERS - 1, iteration, 0)

    last = ITERS - 1

    def put_f(half, total):
        for m in range(8):
            there = half * 8 + m
            f_part[there // 4, there % 4 : there % 4 + 1, :] = norm_x[there] - total[m : m + 1, :]

    put_f(0, merged_f(last, 0))
    target_first()
    put_f(1, merged_f(last, 1))
    f_all[zl] = f_part[y]
    for p in range(1, 4):
        device = place((z // 4) * 4 + (zl + p) % 4, y, x, c)
        remote(f_part.at[y], f_all.at[zl], o_send.at[0], o_recv.at[0], device)

    def last_half(half, carry):
        for i, row in enumerate(target_second(half)):
            part_e[half * 2 + i // 2, i % 2 : i % 2 + 1, :] = row - aux_t[half * 4 + i, 1:2, :]

        def send_e(i, carry):
            y_there = i // 4
            z_there = (i // 2) % 2 * 4 + half * 2 + i % 2

            @pl.when((y_there != y) | (z_there != z))
            def _():
                remote(
                    part_e.at[z_there % 4], recv_e.at[y * 8 + z], e_send.at[0], e_recv.at[0],
                    place(z_there, y_there, x, c),
                )

            return carry

        return lax.fori_loop(0, 16, send_e, carry)

    lax.fori_loop(0, 2, last_half, 0)
    recv_e[y * 8 + z] = part_e[zl]

    arrived(f_all.at[pl.ds(0, 3)], o_recv.at[0])
    for there in range(4):
        f_out[there * 4 : there * 4 + 4, :] = f_all[there]
    arrived(recv_e.at[pl.ds(0, 31)], e_recv.at[0])
    for there in range(4):
        parts = recv_e[there * 8 : there * 8 + 8]
        total = merge(parts[1:], parts[0])
        for half in range(2):
            g_out[half * 4 + there : half * 4 + there + 1, :] = -total[half : half + 1, :]

    arrived(aux_t.at[pl.ds(0, 7)], send_sem.at[0])
    arrived(Y.at[pl.ds(0, 7)], send_sem.at[1])
    arrived(X.at[pl.ds(0, 15), pl.ds(0, 64)], send_sem.at[2])
    arrived(aux_s.at[pl.ds(0, 15)], send_sem.at[3])
    arrived(X.at[pl.ds(0, 16), pl.ds(0, 64)], send_sem.at[4])
    for step in range(ITERS):
        for half in range(2):
            arrived(recv_f.at[step, half], f_send.at[step, half])
            if step < last:
                arrived(recv_g.at[step, half], g_send.at[step, half])
    arrived(f_all.at[pl.ds(0, 3)], o_send.at[0])
    arrived(recv_e.at[pl.ds(0, 31)], e_send.at[0])


def local(source_points, target_points, source_mass, target_mass):
    f32, bf16 = jnp.float32, jnp.bfloat16
    dma = pltpu.SemaphoreType.DMA
    f_scaled, g_scaled = pl.pallas_call(
        kernel,
        out_shape=(jax.ShapeDtypeStruct((16, 128), f32), jax.ShapeDtypeStruct((8, 128), f32)),
        in_specs=[pl.BlockSpec(memory_space=pl.ANY)] * 4,
        out_specs=[pl.BlockSpec(memory_space=pltpu.VMEM)] * 2,
        scratch_shapes=[
            pltpu.VMEM((TILES, 128, 128), bf16),
            pltpu.VMEM((CHUNKS, 128, 128), bf16),
            pltpu.VMEM((CHUNKS, TILES, 128, 128), f32),
            pltpu.VMEM((CHUNKS, 128, 128), f32),
            pltpu.VMEM((TILES, 8, 128), f32),
            pltpu.VMEM((TILES, 8, 128), f32),
            pltpu.VMEM((CHUNKS, 128, 128), f32),
            pltpu.VMEM((CHUNKS, 128, 128), f32),
            pltpu.VMEM((16, 128), f32),
            pltpu.VMEM((8, 128), f32),
            pltpu.VMEM((CHUNKS, 2, 128), f32),
            pltpu.VMEM((TILES, 1, 128), f32),
            pltpu.VMEM((2, 8, 128), f32),
            pltpu.VMEM((TILES, 1, 128), f32),
            pltpu.VMEM((2, 8, 128), f32),
            pltpu.VMEM((ITERS, 2, 8, 128), f32),
            pltpu.VMEM((ITERS, 2, 31, 8, 128), f32),
            pltpu.VMEM((ITERS - 1, 2, 4, 128), f32),
            pltpu.VMEM((ITERS - 1, 2, 7, 4, 128), f32),
            pltpu.VMEM((4, 4, 128), f32),
            pltpu.VMEM((4, 4, 128), f32),
            pltpu.VMEM((4, 2, 128), f32),
            pltpu.VMEM((32, 2, 128), f32),
            dma((4,)),
            dma((TILES,)),
            dma((TILES,)),
            dma((CHUNKS,)),
            dma((1,)),
            dma((1,)),
            dma((5,)),
            dma((ITERS, 2)),
            dma((ITERS, 2)),
            dma((ITERS - 1, 2)),
            dma((ITERS - 1, 2)),
            dma((1,)),
            dma((1,)),
            dma((1,)),
            dma((1,)),
        ],
        compiler_params=pltpu.CompilerParams(collective_id=0, has_side_effects=True, vmem_limit_bytes=VMEM_LIMIT),
    )(source_points, target_points, source_mass.reshape(16, 128), target_mass.reshape(8, 128))
    return f_scaled.reshape(2048) * (1.0 / ALPHA), g_scaled.reshape(1024) * (1.0 / ALPHA)


def solution(mesh):
    placed = (P(("src", "tgt"), None), P(("tgt", "src"), None), P("src"), P("tgt"))
    return jax.shard_map(
        local, mesh=mesh, in_specs=placed, out_specs=(P("src"), P("tgt")), check_vma=False
    )
```

```python
import math

import jax
import jax.numpy as jnp
from jax import lax
from jax.experimental import pallas as pl
from jax.experimental.pallas import tpu as pltpu
from jax.sharding import PartitionSpec as P

MESH = pl.DeviceIdType.MESH

ITERS = 3
EPS = 0.05
ALPHA = 1.0 / (EPS * math.log(2.0))
INV_LN2 = 1.0 / math.log(2.0)

TILES = 16
CHUNKS = 8
LINE = (4, 3, 5, 2, 6, 1, 7)
ORDER = (1, 7, 2, 6, 3, 5, 4)
SETS = ((0, 1, 7, 2), (6, 3, 5, 4))
PLANE = sorted(
    ((dy, dx, dc) for dy in range(4) for dx in range(4) for dc in range(2) if dy or dx or dc),
    key=lambda p: -min(p[0], 4 - p[0]) - min(p[1], 4 - p[1]),
)
CHIPS = [p for p in PLANE if p[2] == 0]
VMEM_LIMIT = 24 * 2**20


def log2(value):
    return jnp.log(value) * INV_LN2


def place(z, y, x, c):
    return {"src": (z // 4) * 4 + y, "tgt": (z % 4) * 8 + x * 2 + c}


def chunk_of(z):
    return (z % 4) * 2 + z // 4


def row_norm(points):
    values = points.astype(jnp.float32)
    square = values * values
    high = square.astype(jnp.bfloat16)
    low = (square - high.astype(jnp.float32)).astype(jnp.bfloat16)
    ones = jnp.ones((8, 128), jnp.bfloat16)
    dims = (((1,), (1,)), ((), ()))
    total = lax.dot_general(ones, high, dims, preferred_element_type=jnp.float32) + lax.dot_general(
        ones, low, dims, preferred_element_type=jnp.float32
    )
    return (0.5 * ALPHA) * total[0:1, :]


def to_column(row):
    return jnp.transpose(jnp.broadcast_to(row, (128, 128)))


def tree(op, values):
    values = list(values)
    while len(values) > 1:
        values = [op(*values[i : i + 2]) if i + 1 < len(values) else values[i] for i in range(0, len(values), 2)]
    return values[0]


def stats(pieces):
    peak = tree(jnp.maximum, pieces)
    return peak, tree(jnp.add, [jnp.exp2(piece - peak) for piece in pieces])


def join(first, second):
    peak = jnp.maximum(first[0], second[0])
    return peak, first[1] * jnp.exp2(first[0] - peak) + second[1] * jnp.exp2(second[0] - peak)


def merge(parts, own):
    top = jnp.maximum(jnp.max(parts, axis=0), own)
    return top + log2(jnp.sum(jnp.exp2(parts - top[None]), axis=0) + jnp.exp2(own - top))


def kernel(
    xs, ys, am, bm, f_out, g_out,
    X, Y, ST, CB, GM, GT, PM, PT, amv, bmv, aux_t, aux_s, logs_a, norm_x, r_rows,
    part_f, recv_f, part_g, recv_g, f_part, f_all, part_e, recv_e,
    local_sem, x_recv, fwd_recv, y_recv, at_recv, as_recv, send_sem,
    f_send, f_recv, g_send, g_recv, o_send, o_recv, e_send, e_recv,
):
    s = lax.axis_index("src")
    t = lax.axis_index("tgt")
    z = (s // 4) * 4 + t // 8
    y = s % 4
    x = (t // 2) % 4
    c = t % 2
    zl = z % 4
    tile = y * 4 + x
    q = chunk_of(z)

    z_at = [(z + p) % 8 for p in range(8)]
    src_z = [there // 4 * 4 for there in z_at]
    tgt_z = [there % 4 * 8 for there in z_at]
    y_at = [(y + p) % 4 for p in range(4)]
    tgt_x = [(x + p) % 4 * 2 for p in range(4)]
    tgt_c = [c, 1 - c]
    tgt_xc = [[tgt_z[0] + tgt_x[p] + tgt_c[r] for r in range(2)] for p in range(4)]
    src_y = [src_z[0] + y_at[p] for p in range(4)]
    tgt_own = tgt_x[0] + c

    def line(p):
        return {"src": src_z[p] + y, "tgt": tgt_z[p] + tgt_own}

    def plane(p):
        return {"src": src_y[p[0]], "tgt": tgt_xc[p[1]][p[2]]}

    sibling = plane((0, 0, 1))

    copies = [
        pltpu.make_async_copy(ys, Y.at[q], local_sem.at[0]),
        pltpu.make_async_copy(xs, X.at[tile, pl.ds(c * 64, 64)], local_sem.at[1]),
        pltpu.make_async_copy(bm, bmv, local_sem.at[2]),
        pltpu.make_async_copy(am, amv, local_sem.at[3]),
    ]
    for copy in copies:
        copy.start()

    barrier = pltpu.get_barrier_semaphore()

    for p in LINE:
        pl.semaphore_signal(barrier, inc=1, device_id=line(p), device_id_type=MESH)
    for p in PLANE:
        pl.semaphore_signal(barrier, inc=1, device_id=plane(p), device_id_type=MESH)

    for copy in copies:
        copy.wait()
    norm = row_norm(Y[q])
    aux_t[q, 0:1, :] = log2(bmv[pl.ds(s, 1), :]) - norm
    aux_t[q, 1:2, :] = norm
    aux_s[tile] = log2(amv[pl.ds(t // 2, 1), :])

    pl.semaphore_wait(barrier, 7 + 31)

    def remote(src, dst, send, recv, device):
        pltpu.make_async_remote_copy(
            src_ref=src, dst_ref=dst, send_sem=send, recv_sem=recv, device_id=device, device_id_type=MESH
        ).start()

    def arrived(ref, sem):
        pltpu.make_async_copy(ref, ref, sem).wait()

    own = (tile, pl.ds(c * 64, 64))
    for p in LINE:
        remote(aux_t.at[q], aux_t.at[q], send_sem.at[0], at_recv.at[0], line(p))
    for p in ORDER:
        remote(Y.at[q], Y.at[q], send_sem.at[1], y_recv.at[q], line(p))
    for p in CHIPS:
        remote(X.at[own], X.at[own], send_sem.at[2], x_recv.at[tile], plane(p))
    remote(X.at[own], X.at[own], send_sem.at[4], fwd_recv.at[tile], sibling)
    for p in CHIPS:
        remote(aux_s.at[tile], aux_s.at[tile], send_sem.at[3], as_recv.at[0], plane(p))

    def row_of(n):
        return (y + (n + 1) // 2 * (2 * (n % 2) - 1) + 4) % 4

    def forward(n):
        for x_there in range(4):
            there = row_of(n) * 4 + x_there
            block = (there, pl.ds(c * 64, 64))

            @pl.when(there != tile)
            def _():
                arrived(X.at[block], x_recv.at[there])
                remote(X.at[block], X.at[block], send_sem.at[4], fwd_recv.at[there], sibling)

    def send_f(step, half):
        for i, p in enumerate(PLANE):
            remote(
                part_f.at[step, half], recv_f.at[step, half, i], f_send.at[step, half], f_recv.at[step, half], plane(p)
            )

    def finish_sources(step, half):
        peaks = GM[pl.ds(half * 8, 8)]
        top = jnp.max(peaks, axis=1)
        total = jnp.sum(GT[pl.ds(half * 8, 8)] * jnp.exp2(peaks - top[:, None, :]), axis=1)
        part_f[step, half] = top + log2(total)
        send_f(step, half)

    def scores(first, count, chunks, add):
        rows = jnp.concatenate([Y[k] for k in chunks], axis=0)
        tiles = X[pl.ds(first, count)].reshape(count * 128, 128)
        product = lax.dot_general(rows, tiles, (((1,), (1,)), ((), ())), preferred_element_type=jnp.float32)
        for m in range(count):
            found = []
            for u, k in enumerate(chunks):
                pieces = []
                for j in range(16):
                    piece = ALPHA * product[(u * 16 + j) * 8 : (u * 16 + j + 1) * 8, m * 128 : (m + 1) * 128]
                    ST[k, first + m, j * 8 : j * 8 + 8, :] = piece
                    pieces.append(piece + CB[k, j * 8 : j * 8 + 8, :])
                found.append(stats(pieces))
            if add:
                found.append((GM[first + m], GT[first + m]))
            GM[first + m], GT[first + m] = tree(join, found)

    def chunks_at(distances):
        return [chunk_of(z_at[p]) for p in distances]

    for n in range(3):
        forward(n)
    arrived(aux_t.at[pl.ds(0, 7)], at_recv.at[0])
    for k in range(CHUNKS):
        CB[k] = to_column(aux_t[k, 0:1, :])
    for k in chunks_at(SETS[0])[1:]:
        arrived(Y.at[k], y_recv.at[k])

    def early(n, carry):
        @pl.when(n == 1)
        def _():
            forward(3)

        row = row_of(n)
        for x_there in range(4):
            there = row * 4 + x_there
            arrived(X.at[there, pl.ds((1 - c) * 64, 64)], fwd_recv.at[there])
        scores(row * 4, 4, chunks_at(SETS[0]), False)
        return carry

    lax.fori_loop(0, 4, early, 0)
    for k in chunks_at(SETS[1]):
        arrived(Y.at[k], y_recv.at[k])

    def late(half, carry):
        scores(half * 8, 8, chunks_at(SETS[1]), True)
        finish_sources(0, half)
        return carry

    lax.fori_loop(0, 2, late, 0)

    arrived(aux_s.at[pl.ds(0, 15)], as_recv.at[0])
    for half in range(2):
        logs_a[half] = jnp.concatenate([aux_s[half * 8 + m] for m in range(8)], axis=0)

    def norms(m, carry):
        norm_x[m] = row_norm(X[m])
        return carry

    lax.fori_loop(0, TILES, norms, 0)

    def merged_f(step, half):
        arrived(recv_f.at[step, half], f_recv.at[step, half])
        total = merge(recv_f[step, half], part_f[step, half])
        r_rows[half] = logs_a[half] - total
        return total

    def target_pieces(k, j, half):
        return [
            ST[k, half * 8 + m, j * 8 : j * 8 + 8, :] + r_rows[half, m : m + 1, :] for m in range(8)
        ]

    def target_first():
        def chunk(k, carry):
            for j in range(16):
                rows = slice(j * 8, j * 8 + 8)
                PM[k, rows, :], PT[k, rows, :] = stats(target_pieces(k, j, 0))
            return carry

        lax.fori_loop(0, CHUNKS, chunk, 0)

    def target_second(half):
        def chunk(i, carry):
            k = half * 4 + i
            for j in range(16):
                rows = slice(j * 8, j * 8 + 8)
                PM[k, rows, :], PT[k, rows, :] = join((PM[k, rows, :], PT[k, rows, :]), stats(target_pieces(k, j, 1)))
            return carry

        lax.fori_loop(0, 4, chunk, 0)
        results = []
        for i in range(4):
            peak, total = jnp.transpose(PM[half * 4 + i]), jnp.transpose(PT[half * 4 + i])
            top = jnp.max(peak, axis=0, keepdims=True)
            results.append(top + log2(jnp.sum(total * jnp.exp2(peak - top), axis=0, keepdims=True)))
        return results

    def merged_g(step, half):
        arrived(recv_g.at[step, half], g_recv.at[step, half])
        total = merge(recv_g[step, half], part_g[step, half])
        for i in range(4):
            k = half * 4 + i
            CB[k] = to_column(aux_t[k, 0:1, :] + aux_t[k, 1:2, :] - total[i : i + 1, :])

    def source_tiles(first, half):
        for u in range(4):
            m = first + u
            for k in range(half * 4, half * 4 + 4):
                found = stats(
                    [ST[k, m, j * 8 : j * 8 + 8, :] + CB[k, j * 8 : j * 8 + 8, :] for j in range(16)]
                )
                state = found if k == half * 4 else join(state, found)
            if half == 1:
                state = join((GM[m], GT[m]), state)
            GM[m], GT[m] = state

    def iteration(step, carry):
        merged_f(step, 0)
        target_first()
        merged_f(step, 1)

        def target_half(half, carry):
            for i, row in enumerate(target_second(half)):
                part_g[step, half, i : i + 1, :] = row

            for i, p in enumerate(LINE):
                remote(
                    part_g.at[step, half], recv_g.at[step, half, i], g_send.at[step, half], g_recv.at[step, half], line(p)
                )
            return carry

        lax.fori_loop(0, 2, target_half, 0)

        merged_g(step, 0)

        def first_tiles(i, carry):
            source_tiles(i * 4, 0)
            return carry

        lax.fori_loop(0, 4, first_tiles, 0)
        merged_g(step, 1)

        def source_half(half, carry):
            def more_tiles(i, carry):
                source_tiles(half * 8 + i * 4, 1)
                return carry

            lax.fori_loop(0, 2, more_tiles, 0)
            finish_sources(step + 1, half)
            return carry

        return lax.fori_loop(0, 2, source_half, carry)

    lax.fori_loop(0, ITERS - 1, iteration, 0)

    last = ITERS - 1

    def put_f(half, total):
        for m in range(8):
            there = half * 8 + m
            f_part[there // 4, there % 4 : there % 4 + 1, :] = norm_x[there] - total[m : m + 1, :]

    put_f(0, merged_f(last, 0))
    target_first()
    put_f(1, merged_f(last, 1))
    f_all[zl] = f_part[y]
    for p in range(1, 4):
        device = place((z // 4) * 4 + (zl + p) % 4, y, x, c)
        remote(f_part.at[y], f_all.at[zl], o_send.at[0], o_recv.at[0], device)

    def last_half(half, carry):
        for i, row in enumerate(target_second(half)):
            part_e[half * 2 + i // 2, i % 2 : i % 2 + 1, :] = row - aux_t[half * 4 + i, 1:2, :]

        def send_e(i, carry):
            y_there = i // 4
            z_there = (i // 2) % 2 * 4 + half * 2 + i % 2

            @pl.when((y_there != y) | (z_there != z))
            def _():
                remote(
                    part_e.at[z_there % 4], recv_e.at[y * 8 + z], e_send.at[0], e_recv.at[0],
                    place(z_there, y_there, x, c),
                )

            return carry

        return lax.fori_loop(0, 16, send_e, carry)

    lax.fori_loop(0, 2, last_half, 0)
    recv_e[y * 8 + z] = part_e[zl]

    arrived(f_all.at[pl.ds(0, 3)], o_recv.at[0])
    for there in range(4):
        f_out[there * 4 : there * 4 + 4, :] = f_all[there]
    arrived(recv_e.at[pl.ds(0, 31)], e_recv.at[0])
    for there in range(4):
        parts = recv_e[there * 8 : there * 8 + 8]
        total = merge(parts[1:], parts[0])
        for half in range(2):
            g_out[half * 4 + there : half * 4 + there + 1, :] = -total[half : half + 1, :]

    arrived(aux_t.at[pl.ds(0, 7)], send_sem.at[0])
    arrived(Y.at[pl.ds(0, 7)], send_sem.at[1])
    arrived(X.at[pl.ds(0, 15), pl.ds(0, 64)], send_sem.at[2])
    arrived(aux_s.at[pl.ds(0, 15)], send_sem.at[3])
    arrived(X.at[pl.ds(0, 16), pl.ds(0, 64)], send_sem.at[4])
    for step in range(ITERS):
        for half in range(2):
            arrived(recv_f.at[step, half], f_send.at[step, half])
            if step < last:
                arrived(recv_g.at[step, half], g_send.at[step, half])
    arrived(f_all.at[pl.ds(0, 3)], o_send.at[0])
    arrived(recv_e.at[pl.ds(0, 31)], e_send.at[0])


def local(source_points, target_points, source_mass, target_mass):
    f32, bf16 = jnp.float32, jnp.bfloat16
    dma = pltpu.SemaphoreType.DMA
    f_scaled, g_scaled = pl.pallas_call(
        kernel,
        out_shape=(jax.ShapeDtypeStruct((16, 128), f32), jax.ShapeDtypeStruct((8, 128), f32)),
        in_specs=[pl.BlockSpec(memory_space=pl.ANY)] * 4,
        out_specs=[pl.BlockSpec(memory_space=pltpu.VMEM)] * 2,
        scratch_shapes=[
            pltpu.VMEM((TILES, 128, 128), bf16),
            pltpu.VMEM((CHUNKS, 128, 128), bf16),
            pltpu.VMEM((CHUNKS, TILES, 128, 128), f32),
            pltpu.VMEM((CHUNKS, 128, 128), f32),
            pltpu.VMEM((TILES, 8, 128), f32),
            pltpu.VMEM((TILES, 8, 128), f32),
            pltpu.VMEM((CHUNKS, 128, 128), f32),
            pltpu.VMEM((CHUNKS, 128, 128), f32),
            pltpu.VMEM((16, 128), f32),
            pltpu.VMEM((8, 128), f32),
            pltpu.VMEM((CHUNKS, 2, 128), f32),
            pltpu.VMEM((TILES, 1, 128), f32),
            pltpu.VMEM((2, 8, 128), f32),
            pltpu.VMEM((TILES, 1, 128), f32),
            pltpu.VMEM((2, 8, 128), f32),
            pltpu.VMEM((ITERS, 2, 8, 128), f32),
            pltpu.VMEM((ITERS, 2, 31, 8, 128), f32),
            pltpu.VMEM((ITERS - 1, 2, 4, 128), f32),
            pltpu.VMEM((ITERS - 1, 2, 7, 4, 128), f32),
            pltpu.VMEM((4, 4, 128), f32),
            pltpu.VMEM((4, 4, 128), f32),
            pltpu.VMEM((4, 2, 128), f32),
            pltpu.VMEM((32, 2, 128), f32),
            dma((4,)),
            dma((TILES,)),
            dma((TILES,)),
            dma((CHUNKS,)),
            dma((1,)),
            dma((1,)),
            dma((5,)),
            dma((ITERS, 2)),
            dma((ITERS, 2)),
            dma((ITERS - 1, 2)),
            dma((ITERS - 1, 2)),
            dma((1,)),
            dma((1,)),
            dma((1,)),
            dma((1,)),
        ],
        compiler_params=pltpu.CompilerParams(collective_id=0, has_side_effects=True, vmem_limit_bytes=VMEM_LIMIT),
    )(*[pltpu.with_memory_space_constraint(v, pltpu.HBM) for v in (source_points, target_points, source_mass.reshape(16, 128), target_mass.reshape(8, 128))])
    return f_scaled.reshape(2048) * (1.0 / ALPHA), g_scaled.reshape(1024) * (1.0 / ALPHA)


def solution(mesh):
    placed = (P(("src", "tgt"), None), P(("tgt", "src"), None), P("src"), P("tgt"))
    return jax.shard_map(
        local, mesh=mesh, in_specs=placed, out_specs=(P("src"), P("tgt")), check_vma=False
    )
```

```python
import math

import jax
import jax.numpy as jnp
from jax import lax
from jax.experimental import pallas as pl
from jax.experimental.pallas import tpu as pltpu
from jax.sharding import PartitionSpec as P

MESH = pl.DeviceIdType.MESH

ITERS = 3
EPS = 0.05
ALPHA = 1.0 / (EPS * math.log(2.0))
INV_LN2 = 1.0 / math.log(2.0)

TILES = 16
CHUNKS = 8
LINE = (4, 3, 5, 2, 6, 1, 7)
ORDER = (2, 6, 3, 5, 1, 7)
SETS = ((0, 1, 7, 2, 6), (3, 5, 4))
PLANE = sorted(
    ((dy, dx, dc) for dy in range(4) for dx in range(4) for dc in range(2) if dy or dx or dc),
    key=lambda p: -min(p[0], 4 - p[0]) - min(p[1], 4 - p[1]),
)
SHEET = sorted(
    ((dy, dz) for dy in range(4) for dz in range(8) if dy or dz), key=lambda p: -min(p[0], 4 - p[0]) - min(p[1], 8 - p[1])
)
CHIPS = [p for p in PLANE if p[2] == 0]
FAR = 9
FAR_CHIPS = [p for p in CHIPS if min(p[0], 4 - p[0]) + min(p[1], 4 - p[1]) >= FAR]
VMEM_LIMIT = 24 * 2**20


def log2(value):
    return jnp.log(value) * INV_LN2


def place(z, y, x, c):
    return {"src": (z // 4) * 4 + y, "tgt": (z % 4) * 8 + x * 2 + c}


def chunk_of(z):
    return (z % 4) * 2 + z // 4


def row_norm(points):
    values = points.astype(jnp.float32)
    square = values * values
    high = square.astype(jnp.bfloat16)
    low = (square - high.astype(jnp.float32)).astype(jnp.bfloat16)
    ones = jnp.ones((8, 128), jnp.bfloat16)
    dims = (((1,), (1,)), ((), ()))
    total = lax.dot_general(ones, high, dims, preferred_element_type=jnp.float32) + lax.dot_general(
        ones, low, dims, preferred_element_type=jnp.float32
    )
    return (0.5 * ALPHA) * total[0:1, :]


def to_column(row):
    return jnp.transpose(jnp.broadcast_to(row, (128, 128)))


def tree(op, values):
    values = list(values)
    while len(values) > 1:
        values = [op(*values[i : i + 2]) if i + 1 < len(values) else values[i] for i in range(0, len(values), 2)]
    return values[0]


def stats(pieces):
    peak = tree(jnp.maximum, pieces)
    return peak, tree(jnp.add, [jnp.exp2(piece - peak) for piece in pieces])


def join(first, second):
    peak = jnp.maximum(first[0], second[0])
    return peak, first[1] * jnp.exp2(first[0] - peak) + second[1] * jnp.exp2(second[0] - peak)


def merge(parts, own):
    top = jnp.maximum(jnp.max(parts, axis=0), own)
    return top + log2(jnp.sum(jnp.exp2(parts - top[None]), axis=0) + jnp.exp2(own - top))


def kernel(
    xs, ys, am, bm, f_out, g_out,
    X, Y, ST, CB, GM, GT, PM, PT, amv, bmv, aux_t, aux_s, logs_a, norm_x, r_rows,
    part_f, recv_f, part_g, recv_g, f_part, f_all, part_e, recv_e,
    local_sem, x_recv, fwd_recv, y_recv, at_recv, as_recv, send_sem,
    f_send, f_recv, g_send, g_recv, o_send, o_recv, e_send, e_recv,
):
    s = lax.axis_index("src")
    t = lax.axis_index("tgt")
    z = (s // 4) * 4 + t // 8
    y = s % 4
    x = (t // 2) % 4
    c = t % 2
    zl = z % 4
    tile = y * 4 + x
    q = chunk_of(z)

    z_at = [(z + p) % 8 for p in range(8)]
    src_z = [there // 4 * 4 for there in z_at]
    tgt_z = [there % 4 * 8 for there in z_at]
    zl_at = [there % 4 for there in z_at]
    y_at = [(y + p) % 4 for p in range(4)]
    x_at = [(x + p) % 4 for p in range(4)]
    tgt_x = [(x + p) % 4 * 2 for p in range(4)]
    tgt_c = [c, 1 - c]
    tgt_xc = [[tgt_z[0] + tgt_x[p] + tgt_c[r] for r in range(2)] for p in range(4)]
    src_y = [src_z[0] + y_at[p] for p in range(4)]
    tgt_own = tgt_x[0] + c

    def line(p):
        return {"src": src_z[p] + y, "tgt": tgt_z[p] + tgt_own}

    def plane(p):
        return {"src": src_y[p[0]], "tgt": tgt_xc[p[1]][p[2]]}

    sibling = plane((0, 0, 1))

    copies = [
        pltpu.make_async_copy(ys, Y.at[q], local_sem.at[0]),
        pltpu.make_async_copy(xs, X.at[tile, pl.ds(c * 64, 64)], local_sem.at[1]),
        pltpu.make_async_copy(bm, bmv, local_sem.at[2]),
        pltpu.make_async_copy(am, amv, local_sem.at[3]),
    ]
    for copy in copies:
        copy.start()

    barrier = pltpu.get_barrier_semaphore()

    for p in LINE:
        pl.semaphore_signal(barrier, inc=1, device_id=line(p), device_id_type=MESH)
    for p in PLANE:
        pl.semaphore_signal(barrier, inc=1, device_id=plane(p), device_id_type=MESH)

    for copy in copies:
        copy.wait()
    norm = row_norm(Y[q])
    aux_t[q, 0:1, :] = log2(bmv[pl.ds(s, 1), :]) - norm
    aux_t[q, 1:2, :] = norm
    aux_s[tile] = log2(amv[pl.ds(t // 2, 1), :])

    pl.semaphore_wait(barrier, 7 + 31)

    def remote(src, dst, send, recv, device):
        pltpu.make_async_remote_copy(
            src_ref=src, dst_ref=dst, send_sem=send, recv_sem=recv, device_id=device, device_id_type=MESH
        ).start()

    def arrived(ref, sem):
        pltpu.make_async_copy(ref, ref, sem).wait()

    own = (tile, pl.ds(c * 64, 64))
    for p in LINE:
        remote(aux_t.at[q], aux_t.at[q], send_sem.at[0], at_recv.at[0], line(p))
    for p in ORDER:
        remote(Y.at[q], Y.at[q], send_sem.at[1], y_recv.at[q], line(p))
    for p in CHIPS:
        remote(X.at[own], X.at[own], send_sem.at[2], x_recv.at[tile], plane(p))
    for dy, dx, _ in FAR_CHIPS:
        remote(X.at[own], X.at[own], send_sem.at[4], fwd_recv.at[tile], plane((dy, dx, 1)))
    remote(X.at[own], X.at[own], send_sem.at[4], fwd_recv.at[tile], sibling)
    for p in CHIPS:
        remote(aux_s.at[tile], aux_s.at[tile], send_sem.at[3], as_recv.at[0], plane(p))

    def row_of(n):
        return (y + (n + 1) // 2 * (2 * (n % 2) - 1) + 4) % 4

    def forward(n):
        dy = (0, 1, 3, 2)[n]
        for dx in (0, 1, 3, 2):
            if (dy, dx) != (0, 0) and (dy, dx, 0) not in FAR_CHIPS:
                there = y_at[dy] * 4 + x_at[dx]
                block = (there, pl.ds(c * 64, 64))
                arrived(X.at[block], x_recv.at[there])
                remote(X.at[block], X.at[block], send_sem.at[4], fwd_recv.at[there], sibling)

    def send_f(step, half):
        for i, p in enumerate(PLANE):
            remote(
                part_f.at[step, half], recv_f.at[step, half, i], f_send.at[step, half], f_recv.at[step, half], plane(p)
            )

    def finish_sources(step, half):
        peaks = GM[pl.ds(half * 8, 8)]
        top = jnp.max(peaks, axis=1)
        total = jnp.sum(GT[pl.ds(half * 8, 8)] * jnp.exp2(peaks - top[:, None, :]), axis=1)
        part_f[step, half] = top + log2(total)
        send_f(step, half)

    def scores(first, count, chunks, add):
        rows = jnp.concatenate([Y[k] for k in chunks], axis=0)
        tiles = X[pl.ds(first, count)].reshape(count * 128, 128)
        product = lax.dot_general(rows, tiles, (((1,), (1,)), ((), ())), preferred_element_type=jnp.float32)
        for m in range(count):
            found = []
            for u, k in enumerate(chunks):
                pieces = []
                for j in range(16):
                    piece = ALPHA * product[(u * 16 + j) * 8 : (u * 16 + j + 1) * 8, m * 128 : (m + 1) * 128]
                    ST[k, first + m, j * 8 : j * 8 + 8, :] = piece
                    pieces.append(piece + CB[k, j * 8 : j * 8 + 8, :])
                found.append(stats(pieces))
            if add:
                found.append((GM[first + m], GT[first + m]))
            GM[first + m], GT[first + m] = tree(join, found)

    def chunks_at(distances):
        return [chunk_of(z_at[p]) for p in distances]

    for n in range(3):
        forward(n)
        if n == 0:
            for p, rows in ((2, pl.ds(0, 64)), (6, pl.ds(64, 64))):
                k = chunk_of(z_at[p])
                arrived(Y.at[k], y_recv.at[k])
                remote(Y.at[k, rows], Y.at[k, rows], send_sem.at[5], y_recv.at[k], line(8 - p))
    arrived(aux_t.at[pl.ds(0, 7)], at_recv.at[0])
    for k in range(CHUNKS):
        CB[k] = to_column(aux_t[k, 0:1, :])
    forward(3)
    for k in chunks_at(p for p in SETS[0] if p not in (0, 2, 6)):
        arrived(Y.at[k], y_recv.at[k])

    def hops(n, x_there):
        dx = (x_there - x + 4) % 4
        return (n + 1) // 2 + dx - dx // 3 * 2

    def early(n, carry):
        row = row_of(n)
        for x_there in range(4):
            there = row * 4 + x_there
            arrived(X.at[there, pl.ds((1 - c) * 64, 64)], fwd_recv.at[there])

            @pl.when(hops(n, x_there) >= FAR)
            def _():
                arrived(X.at[there, pl.ds(c * 64, 64)], x_recv.at[there])

        scores(row * 4, 4, chunks_at(SETS[0]), False)
        return carry

    lax.fori_loop(0, 4, early, 0)
    for k in chunks_at(p for p in SETS[1] if p not in (0, 2, 6)):
        arrived(Y.at[k], y_recv.at[k])

    def late(half, carry):
        scores(half * 8, 8, chunks_at(SETS[1]), True)
        finish_sources(0, half)
        return carry

    lax.fori_loop(0, 2, late, 0)

    arrived(aux_s.at[pl.ds(0, 15)], as_recv.at[0])
    for half in range(2):
        logs_a[half] = jnp.concatenate([aux_s[half * 8 + m] for m in range(8)], axis=0)

    def norms(m, carry):
        norm_x[m] = row_norm(X[m])
        return carry

    lax.fori_loop(0, TILES, norms, 0)

    def merged_f(step, half):
        arrived(recv_f.at[step, half], f_recv.at[step, half])
        total = merge(recv_f[step, half], part_f[step, half])
        r_rows[half] = logs_a[half] - total
        return total

    def target_pieces(k, j, half):
        return [
            ST[k, half * 8 + m, j * 8 : j * 8 + 8, :] + r_rows[half, m : m + 1, :] for m in range(8)
        ]

    def target_first():
        def chunk(k, carry):
            for j in range(16):
                rows = slice(j * 8, j * 8 + 8)
                PM[k, rows, :], PT[k, rows, :] = stats(target_pieces(k, j, 0))
            return carry

        lax.fori_loop(0, CHUNKS, chunk, 0)

    def target_second(half):
        def chunk(i, carry):
            k = half * 4 + i
            for j in range(16):
                rows = slice(j * 8, j * 8 + 8)
                PM[k, rows, :], PT[k, rows, :] = join((PM[k, rows, :], PT[k, rows, :]), stats(target_pieces(k, j, 1)))
            return carry

        lax.fori_loop(0, 4, chunk, 0)
        results = []
        for i in range(4):
            peak, total = jnp.transpose(PM[half * 4 + i]), jnp.transpose(PT[half * 4 + i])
            top = jnp.max(peak, axis=0, keepdims=True)
            results.append(top + log2(jnp.sum(total * jnp.exp2(peak - top), axis=0, keepdims=True)))
        return results

    def merged_g(step, half):
        arrived(recv_g.at[step, half], g_recv.at[step, half])
        total = merge(recv_g[step, half], part_g[step, half])
        for i in range(4):
            k = half * 4 + i
            CB[k] = to_column(aux_t[k, 0:1, :] + aux_t[k, 1:2, :] - total[i : i + 1, :])

    def source_tiles(first, half):
        for u in range(4):
            m = first + u
            for k in range(half * 4, half * 4 + 4):
                found = stats(
                    [ST[k, m, j * 8 : j * 8 + 8, :] + CB[k, j * 8 : j * 8 + 8, :] for j in range(16)]
                )
                state = found if k == half * 4 else join(state, found)
            if half == 1:
                state = join((GM[m], GT[m]), state)
            GM[m], GT[m] = state

    last = ITERS - 1

    def iteration(step, carry):
        first = merged_f(step, 0)
        target_first()
        second = merged_f(step, 1)

        def target_half(half, carry):
            rows = target_second(half)

            @pl.when(step < last)
            def _():
                for i, row in enumerate(rows):
                    part_g[step, half, i : i + 1, :] = row
                for i, p in enumerate(LINE):
                    remote(
                        part_g.at[step, half], recv_g.at[step, half, i], g_send.at[step, half], g_recv.at[step, half], line(p)
                    )

            @pl.when(step == last)
            def _():
                for i, row in enumerate(rows):
                    part_e[half * 2 + i // 2, i % 2 : i % 2 + 1, :] = row - aux_t[half * 4 + i, 1:2, :]
                for dy, dz in SHEET:

                    @pl.when(zl_at[dz] // 2 == half)
                    def _():
                        remote(
                            part_e.at[zl_at[dz]], recv_e.at[y * 8 + z], e_send.at[0], e_recv.at[0],
                            {"src": src_z[dz] + y_at[dy], "tgt": tgt_z[dz] + tgt_own},
                        )


            return carry

        lax.fori_loop(0, 2, target_half, 0)

        @pl.when(step < last)
        def _():
            merged_g(step, 0)

            def first_tiles(i, carry):
                source_tiles(i * 4, 0)
                return carry

            lax.fori_loop(0, 4, first_tiles, 0)
            merged_g(step, 1)

            def source_half(half, carry):
                def more_tiles(i, carry):
                    source_tiles(half * 8 + i * 4, 1)
                    return carry

                lax.fori_loop(0, 2, more_tiles, 0)
                finish_sources(step + 1, half)
                return carry

            lax.fori_loop(0, 2, source_half, 0)

        @pl.when(step == last)
        def _():
            for half, total in enumerate((first, second)):
                for m in range(8):
                    there = half * 8 + m
                    f_part[there // 4, there % 4 : there % 4 + 1, :] = norm_x[there] - total[m : m + 1, :]

        return carry

    lax.fori_loop(0, ITERS, iteration, 0)

    f_all[zl] = f_part[y]
    for p in range(1, 4):
        device = {"src": src_y[0], "tgt": (zl + p) % 4 * 8 + tgt_own}
        remote(f_part.at[y], f_all.at[zl], o_send.at[0], o_recv.at[0], device)
    recv_e[y * 8 + z] = part_e[zl]

    arrived(f_all.at[pl.ds(0, 3)], o_recv.at[0])
    for there in range(4):
        f_out[there * 4 : there * 4 + 4, :] = f_all[there]
    arrived(recv_e.at[pl.ds(0, 31)], e_recv.at[0])
    for there in range(4):
        parts = recv_e[there * 8 : there * 8 + 8]
        total = merge(parts[1:], parts[0])
        for half in range(2):
            g_out[half * 4 + there : half * 4 + there + 1, :] = -total[half : half + 1, :]

    arrived(aux_t.at[pl.ds(0, 7)], send_sem.at[0])
    arrived(Y.at[pl.ds(0, 6)], send_sem.at[1])
    arrived(Y.at[0], send_sem.at[5])
    arrived(X.at[pl.ds(0, 15), pl.ds(0, 64)], send_sem.at[2])
    arrived(aux_s.at[pl.ds(0, 15)], send_sem.at[3])
    arrived(X.at[pl.ds(0, 16), pl.ds(0, 64)], send_sem.at[4])
    for step in range(ITERS):
        for half in range(2):
            arrived(recv_f.at[step, half], f_send.at[step, half])
            if step < last:
                arrived(recv_g.at[step, half], g_send.at[step, half])
    arrived(f_all.at[pl.ds(0, 3)], o_send.at[0])
    arrived(recv_e.at[pl.ds(0, 31)], e_send.at[0])


def local(source_points, target_points, source_mass, target_mass):
    f32, bf16 = jnp.float32, jnp.bfloat16
    dma = pltpu.SemaphoreType.DMA
    f_scaled, g_scaled = pl.pallas_call(
        kernel,
        out_shape=(jax.ShapeDtypeStruct((16, 128), f32), jax.ShapeDtypeStruct((8, 128), f32)),
        in_specs=[pl.BlockSpec(memory_space=pl.ANY)] * 4,
        out_specs=[pl.BlockSpec(memory_space=pltpu.VMEM)] * 2,
        scratch_shapes=[
            pltpu.VMEM((TILES, 128, 128), bf16),
            pltpu.VMEM((CHUNKS, 128, 128), bf16),
            pltpu.VMEM((CHUNKS, TILES, 128, 128), f32),
            pltpu.VMEM((CHUNKS, 128, 128), f32),
            pltpu.VMEM((TILES, 8, 128), f32),
            pltpu.VMEM((TILES, 8, 128), f32),
            pltpu.VMEM((CHUNKS, 128, 128), f32),
            pltpu.VMEM((CHUNKS, 128, 128), f32),
            pltpu.VMEM((16, 128), f32),
            pltpu.VMEM((8, 128), f32),
            pltpu.VMEM((CHUNKS, 2, 128), f32),
            pltpu.VMEM((TILES, 1, 128), f32),
            pltpu.VMEM((2, 8, 128), f32),
            pltpu.VMEM((TILES, 1, 128), f32),
            pltpu.VMEM((2, 8, 128), f32),
            pltpu.VMEM((ITERS, 2, 8, 128), f32),
            pltpu.VMEM((ITERS, 2, 31, 8, 128), f32),
            pltpu.VMEM((ITERS - 1, 2, 4, 128), f32),
            pltpu.VMEM((ITERS - 1, 2, 7, 4, 128), f32),
            pltpu.VMEM((4, 4, 128), f32),
            pltpu.VMEM((4, 4, 128), f32),
            pltpu.VMEM((4, 2, 128), f32),
            pltpu.VMEM((32, 2, 128), f32),
            dma((4,)),
            dma((TILES,)),
            dma((TILES,)),
            dma((CHUNKS,)),
            dma((1,)),
            dma((1,)),
            dma((6,)),
            dma((ITERS, 2)),
            dma((ITERS, 2)),
            dma((ITERS - 1, 2)),
            dma((ITERS - 1, 2)),
            dma((1,)),
            dma((1,)),
            dma((1,)),
            dma((1,)),
        ],
        compiler_params=pltpu.CompilerParams(collective_id=0, has_side_effects=True, vmem_limit_bytes=VMEM_LIMIT),
    )(*[pltpu.with_memory_space_constraint(v, pltpu.HBM) for v in (source_points, target_points, source_mass.reshape(16, 128), target_mass.reshape(8, 128))])
    return f_scaled.reshape(2048) * (1.0 / ALPHA), g_scaled.reshape(1024) * (1.0 / ALPHA)


def solution(mesh):
    placed = (P(("src", "tgt"), None), P(("tgt", "src"), None), P("src"), P("tgt"))
    return jax.shard_map(
        local, mesh=mesh, in_specs=placed, out_specs=(P("src"), P("tgt")), check_vma=False
    )
```

```python
import math

import jax
import jax.numpy as jnp
from jax import lax
from jax.experimental import pallas as pl
from jax.experimental.pallas import tpu as pltpu
from jax.sharding import PartitionSpec as P

MESH = pl.DeviceIdType.MESH

ITERS = 3
EPS = 0.05
ALPHA = 1.0 / (EPS * math.log(2.0))
INV_LN2 = 1.0 / math.log(2.0)

TILES = 16
CHUNKS = 8
LINE = (4, 3, 5, 2, 6, 1, 7)
ORDER = (2, 6, 3, 5, 1, 7)
SETS = ((0, 1, 7, 2, 6), (3, 5, 4))
PLANE = sorted(
    ((dy, dx, dc) for dy in range(4) for dx in range(4) for dc in range(2) if dy or dx or dc),
    key=lambda p: -min(p[0], 4 - p[0]) - min(p[1], 4 - p[1]),
)
SHEET = sorted(
    ((dy, dz) for dy in range(4) for dz in range(8) if dy or dz), key=lambda p: -min(p[0], 4 - p[0]) - min(p[1], 8 - p[1])
)
CHIPS = [p for p in PLANE if p[2] == 0]
FAR = 9
FAR_CHIPS = [p for p in CHIPS if min(p[0], 4 - p[0]) + min(p[1], 4 - p[1]) >= FAR]
VMEM_LIMIT = 24 * 2**20


def log2(value):
    return jnp.log(value) * INV_LN2


def place(z, y, x, c):
    return {"src": (z // 4) * 4 + y, "tgt": (z % 4) * 8 + x * 2 + c}


def chunk_of(z):
    return (z % 4) * 2 + z // 4


def row_norm(points):
    values = points.astype(jnp.float32)
    square = values * values
    high = square.astype(jnp.bfloat16)
    low = (square - high.astype(jnp.float32)).astype(jnp.bfloat16)
    ones = jnp.ones((8, 128), jnp.bfloat16)
    dims = (((1,), (1,)), ((), ()))
    total = lax.dot_general(ones, high, dims, preferred_element_type=jnp.float32) + lax.dot_general(
        ones, low, dims, preferred_element_type=jnp.float32
    )
    return (0.5 * ALPHA) * total[0:1, :]


def to_column(row):
    return jnp.transpose(jnp.broadcast_to(row, (128, 128)))


def tree(op, values):
    values = list(values)
    while len(values) > 1:
        values = [op(*values[i : i + 2]) if i + 1 < len(values) else values[i] for i in range(0, len(values), 2)]
    return values[0]


def stats(pieces):
    peak = tree(jnp.maximum, pieces)
    return peak, tree(jnp.add, [jnp.exp2(piece - peak) for piece in pieces])


def join(first, second):
    peak = jnp.maximum(first[0], second[0])
    return peak, first[1] * jnp.exp2(first[0] - peak) + second[1] * jnp.exp2(second[0] - peak)


def merge(parts, own):
    top = jnp.maximum(jnp.max(parts, axis=0), own)
    return top + log2(jnp.sum(jnp.exp2(parts - top[None]), axis=0) + jnp.exp2(own - top))


def kernel(
    xs, ys, am, bm, f_out, g_out,
    X, Y, ST, CB, GM, GT, PM, PT, amv, bmv, aux_t, aux_s, logs_a, norm_x, r_rows,
    part_f, recv_f, part_g, recv_g, f_part, f_all, part_e, recv_e,
    local_sem, x_recv, fwd_recv, y_recv, at_recv, as_recv, send_sem,
    f_send, f_recv, g_send, g_recv, o_send, o_recv, e_send, e_recv,
):
    s = lax.axis_index("src")
    t = lax.axis_index("tgt")
    z = (s // 4) * 4 + t // 8
    y = s % 4
    x = (t // 2) % 4
    c = t % 2
    zl = z % 4
    tile = y * 4 + x
    q = chunk_of(z)

    z_at = [(z + p) % 8 for p in range(8)]
    src_z = [there // 4 * 4 for there in z_at]
    tgt_z = [there % 4 * 8 for there in z_at]
    zl_at = [there % 4 for there in z_at]
    y_at = [(y + p) % 4 for p in range(4)]
    x_at = [(x + p) % 4 for p in range(4)]
    tgt_x = [(x + p) % 4 * 2 for p in range(4)]
    tgt_c = [c, 1 - c]
    tgt_xc = [[tgt_z[0] + tgt_x[p] + tgt_c[r] for r in range(2)] for p in range(4)]
    src_y = [src_z[0] + y_at[p] for p in range(4)]
    tgt_own = tgt_x[0] + c

    def line(p):
        return {"src": src_z[p] + y, "tgt": tgt_z[p] + tgt_own}

    def plane(p):
        return {"src": src_y[p[0]], "tgt": tgt_xc[p[1]][p[2]]}

    sibling = plane((0, 0, 1))

    copies = [
        pltpu.make_async_copy(ys, Y.at[q], local_sem.at[0]),
        pltpu.make_async_copy(xs, X.at[tile, pl.ds(c * 64, 64)], local_sem.at[1]),
        pltpu.make_async_copy(bm, bmv, local_sem.at[2]),
        pltpu.make_async_copy(am, amv, local_sem.at[3]),
    ]
    for copy in copies:
        copy.start()

    barrier = pltpu.get_barrier_semaphore()

    for p in LINE:
        pl.semaphore_signal(barrier, inc=1, device_id=line(p), device_id_type=MESH)
    for p in PLANE:
        pl.semaphore_signal(barrier, inc=1, device_id=plane(p), device_id_type=MESH)

    for copy in copies:
        copy.wait()
    norm = row_norm(Y[q])
    aux_t[q, 0:1, :] = log2(bmv[pl.ds(s, 1), :]) - norm
    aux_t[q, 1:2, :] = norm
    aux_s[tile] = log2(amv[pl.ds(t // 2, 1), :])

    pl.semaphore_wait(barrier, 7 + 31)

    def remote(src, dst, send, recv, device):
        pltpu.make_async_remote_copy(
            src_ref=src, dst_ref=dst, send_sem=send, recv_sem=recv, device_id=device, device_id_type=MESH
        ).start()

    def arrived(ref, sem):
        pltpu.make_async_copy(ref, ref, sem).wait()

    own = (tile, pl.ds(c * 64, 64))
    for p in LINE:
        remote(aux_t.at[q], aux_t.at[q], send_sem.at[0], at_recv.at[0], line(p))
    for p in ORDER:
        remote(Y.at[q], Y.at[q], send_sem.at[1], y_recv.at[q], line(p))
    for p in CHIPS:
        remote(X.at[own], X.at[own], send_sem.at[2], x_recv.at[tile], plane(p))
    for dy, dx, _ in FAR_CHIPS:
        remote(X.at[own], X.at[own], send_sem.at[4], fwd_recv.at[tile], plane((dy, dx, 1)))
    remote(X.at[own], X.at[own], send_sem.at[4], fwd_recv.at[tile], sibling)
    for p in CHIPS:
        remote(aux_s.at[tile], aux_s.at[tile], send_sem.at[3], as_recv.at[0], plane(p))

    def row_of(n):
        return (y + (n + 1) // 2 * (2 * (n % 2) - 1) + 4) % 4

    def forward(n):
        dy = (0, 1, 3, 2)[n]
        for dx in (0, 1, 3, 2):
            if (dy, dx) != (0, 0) and (dy, dx, 0) not in FAR_CHIPS:
                there = y_at[dy] * 4 + x_at[dx]
                block = (there, pl.ds(c * 64, 64))
                arrived(X.at[block], x_recv.at[there])
                remote(X.at[block], X.at[block], send_sem.at[4], fwd_recv.at[there], sibling)

    def send_f(step, half):
        for i, p in enumerate(PLANE):
            remote(
                part_f.at[step, half], recv_f.at[step, half, i], f_send.at[step, half], f_recv.at[step, half], plane(p)
            )

    def finish_sources(step, half):
        peaks = GM[pl.ds(half * 8, 8)]
        top = jnp.max(peaks, axis=1)
        total = jnp.sum(GT[pl.ds(half * 8, 8)] * jnp.exp2(peaks - top[:, None, :]), axis=1)
        part_f[step, half] = top + log2(total)
        send_f(step, half)

    def scores(first, count, chunks, add):
        rows = jnp.concatenate([Y[k] for k in chunks], axis=0)
        tiles = X[pl.ds(first, count)].reshape(count * 128, 128)
        product = lax.dot_general(rows, tiles, (((1,), (1,)), ((), ())), preferred_element_type=jnp.float32)
        for m in range(count):
            found = []
            for u, k in enumerate(chunks):
                pieces = []
                for j in range(16):
                    piece = ALPHA * product[(u * 16 + j) * 8 : (u * 16 + j + 1) * 8, m * 128 : (m + 1) * 128]
                    ST[k, first + m, j * 8 : j * 8 + 8, :] = piece
                    pieces.append(piece + CB[k, j * 8 : j * 8 + 8, :])
                found.append(stats(pieces))
            if add:
                found.append((GM[first + m], GT[first + m]))
            GM[first + m], GT[first + m] = tree(join, found)

    def chunks_at(distances):
        return [chunk_of(z_at[p]) for p in distances]

    for n in range(3):
        forward(n)
        if n == 0:
            for p, rows in ((2, pl.ds(0, 64)), (6, pl.ds(64, 64))):
                k = chunk_of(z_at[p])
                arrived(Y.at[k], y_recv.at[k])
                remote(Y.at[k, rows], Y.at[k, rows], send_sem.at[5], y_recv.at[k], line(8 - p))
    arrived(aux_t.at[pl.ds(0, 7)], at_recv.at[0])
    for k in range(CHUNKS):
        CB[k] = to_column(aux_t[k, 0:1, :])
    forward(3)
    for k in chunks_at(p for p in SETS[0] if p not in (0, 2, 6)):
        arrived(Y.at[k], y_recv.at[k])

    def hops(n, x_there):
        dx = (x_there - x + 4) % 4
        return (n + 1) // 2 + dx - dx // 3 * 2

    def early(n, carry):
        row = row_of(n)
        for x_there in range(4):
            there = row * 4 + x_there
            arrived(X.at[there, pl.ds((1 - c) * 64, 64)], fwd_recv.at[there])

            @pl.when(hops(n, x_there) >= FAR)
            def _():
                arrived(X.at[there, pl.ds(c * 64, 64)], x_recv.at[there])

        scores(row * 4, 4, chunks_at(SETS[0]), False)
        return carry

    lax.fori_loop(0, 4, early, 0)
    for k in chunks_at(p for p in SETS[1] if p not in (0, 2, 6)):
        arrived(Y.at[k], y_recv.at[k])

    def late(half, carry):
        scores(half * 8, 8, chunks_at(SETS[1]), True)
        finish_sources(0, half)
        return carry

    lax.fori_loop(0, 2, late, 0)

    arrived(aux_s.at[pl.ds(0, 15)], as_recv.at[0])
    for half in range(2):
        logs_a[half] = jnp.concatenate([aux_s[half * 8 + m] for m in range(8)], axis=0)

    def norms(m, carry):
        norm_x[m] = row_norm(X[m])
        return carry

    lax.fori_loop(0, TILES, norms, 0)

    def merged_f(step, half):
        arrived(recv_f.at[step, half], f_recv.at[step, half])
        total = merge(recv_f[step, half], part_f[step, half])
        r_rows[half] = logs_a[half] - total
        return total

    def target_pieces(k, j, half):
        return [
            ST[k, half * 8 + m, j * 8 : j * 8 + 8, :] + r_rows[half, m : m + 1, :] for m in range(8)
        ]

    def target_first():
        def chunk(i, carry):
            for k in (i * 2, i * 2 + 1):
                for j in range(16):
                    rows = slice(j * 8, j * 8 + 8)
                    PM[k, rows, :], PT[k, rows, :] = stats(target_pieces(k, j, 0))
            return carry

        lax.fori_loop(0, CHUNKS // 2, chunk, 0)

    def target_second(half):
        results = []
        for i in range(4):
            k = half * 4 + i
            values = []
            for j in range(16):
                rows = slice(j * 8, j * 8 + 8)
                found = join((PM[k, rows, :], PT[k, rows, :]), stats(target_pieces(k, j, 1)))
                values.append(found[0] + log2(found[1]))
            turned = jnp.transpose(jnp.concatenate(values, axis=0))
            top = jnp.max(turned, axis=0, keepdims=True)
            results.append(top + log2(jnp.sum(jnp.exp2(turned - top), axis=0, keepdims=True)))
        return results

    def merged_g(step, half):
        arrived(recv_g.at[step, half], g_recv.at[step, half])
        total = merge(recv_g[step, half], part_g[step, half])
        for i in range(4):
            k = half * 4 + i
            CB[k] = to_column(aux_t[k, 0:1, :] + aux_t[k, 1:2, :] - total[i : i + 1, :])

    def source_tiles(first, half):
        for u in range(4):
            m = first + u
            for k in range(half * 4, half * 4 + 4):
                found = stats(
                    [ST[k, m, j * 8 : j * 8 + 8, :] + CB[k, j * 8 : j * 8 + 8, :] for j in range(16)]
                )
                state = found if k == half * 4 else join(state, found)
            if half == 1:
                state = join((GM[m], GT[m]), state)
            GM[m], GT[m] = state

    last = ITERS - 1

    def iteration(step, carry):
        first = merged_f(step, 0)
        target_first()
        second = merged_f(step, 1)

        def target_half(half, carry):
            rows = target_second(half)

            @pl.when(step < last)
            def _():
                for i, row in enumerate(rows):
                    part_g[step, half, i : i + 1, :] = row
                for i, p in enumerate(LINE):
                    remote(
                        part_g.at[step, half], recv_g.at[step, half, i], g_send.at[step, half], g_recv.at[step, half], line(p)
                    )

            @pl.when(step == last)
            def _():
                for i, row in enumerate(rows):
                    part_e[half * 2 + i // 2, i % 2 : i % 2 + 1, :] = row - aux_t[half * 4 + i, 1:2, :]
                for dy, dz in SHEET:

                    @pl.when(zl_at[dz] // 2 == half)
                    def _():
                        remote(
                            part_e.at[zl_at[dz]], recv_e.at[y * 8 + z], e_send.at[0], e_recv.at[0],
                            {"src": src_z[dz] + y_at[dy], "tgt": tgt_z[dz] + tgt_own},
                        )


            return carry

        lax.fori_loop(0, 2, target_half, 0)

        @pl.when(step < last)
        def _():
            merged_g(step, 0)

            def first_tiles(i, carry):
                source_tiles(i * 4, 0)
                return carry

            lax.fori_loop(0, 4, first_tiles, 0)
            merged_g(step, 1)

            def source_half(half, carry):
                for i in range(2):
                    source_tiles(half * 8 + i * 4, 1)
                finish_sources(step + 1, half)
                return carry

            lax.fori_loop(0, 2, source_half, 0)

        @pl.when(step == last)
        def _():
            for half, total in enumerate((first, second)):
                for m in range(8):
                    there = half * 8 + m
                    f_part[there // 4, there % 4 : there % 4 + 1, :] = norm_x[there] - total[m : m + 1, :]

        return carry

    lax.fori_loop(0, ITERS, iteration, 0)

    f_all[zl] = f_part[y]
    for p in range(1, 4):
        device = {"src": src_y[0], "tgt": (zl + p) % 4 * 8 + tgt_own}
        remote(f_part.at[y], f_all.at[zl], o_send.at[0], o_recv.at[0], device)
    recv_e[y * 8 + z] = part_e[zl]

    arrived(f_all.at[pl.ds(0, 3)], o_recv.at[0])
    for there in range(4):
        f_out[there * 4 : there * 4 + 4, :] = f_all[there]
    arrived(aux_t.at[pl.ds(0, 7)], send_sem.at[0])
    arrived(Y.at[pl.ds(0, 6)], send_sem.at[1])
    arrived(Y.at[0], send_sem.at[5])
    arrived(X.at[pl.ds(0, 15), pl.ds(0, 64)], send_sem.at[2])
    arrived(aux_s.at[pl.ds(0, 15)], send_sem.at[3])
    arrived(X.at[pl.ds(0, 16), pl.ds(0, 64)], send_sem.at[4])
    for step in range(ITERS):
        for half in range(2):
            arrived(recv_f.at[step, half], f_send.at[step, half])
            if step < last:
                arrived(recv_g.at[step, half], g_send.at[step, half])
    arrived(f_all.at[pl.ds(0, 3)], o_send.at[0])
    arrived(recv_e.at[pl.ds(0, 31)], e_send.at[0])

    arrived(recv_e.at[pl.ds(0, 31)], e_recv.at[0])
    for there in range(4):
        parts = recv_e[there * 8 : there * 8 + 8]
        total = merge(parts[1:], parts[0])
        for half in range(2):
            g_out[half * 4 + there : half * 4 + there + 1, :] = -total[half : half + 1, :]


def local(source_points, target_points, source_mass, target_mass):
    f32, bf16 = jnp.float32, jnp.bfloat16
    dma = pltpu.SemaphoreType.DMA
    f_scaled, g_scaled = pl.pallas_call(
        kernel,
        out_shape=(jax.ShapeDtypeStruct((16, 128), f32), jax.ShapeDtypeStruct((8, 128), f32)),
        in_specs=[pl.BlockSpec(memory_space=pl.ANY)] * 4,
        out_specs=[pl.BlockSpec(memory_space=pltpu.VMEM)] * 2,
        scratch_shapes=[
            pltpu.VMEM((TILES, 128, 128), bf16),
            pltpu.VMEM((CHUNKS, 128, 128), bf16),
            pltpu.VMEM((CHUNKS, TILES, 128, 128), f32),
            pltpu.VMEM((CHUNKS, 128, 128), f32),
            pltpu.VMEM((TILES, 8, 128), f32),
            pltpu.VMEM((TILES, 8, 128), f32),
            pltpu.VMEM((CHUNKS, 128, 128), f32),
            pltpu.VMEM((CHUNKS, 128, 128), f32),
            pltpu.VMEM((16, 128), f32),
            pltpu.VMEM((8, 128), f32),
            pltpu.VMEM((CHUNKS, 2, 128), f32),
            pltpu.VMEM((TILES, 1, 128), f32),
            pltpu.VMEM((2, 8, 128), f32),
            pltpu.VMEM((TILES, 1, 128), f32),
            pltpu.VMEM((2, 8, 128), f32),
            pltpu.VMEM((ITERS, 2, 8, 128), f32),
            pltpu.VMEM((ITERS, 2, 31, 8, 128), f32),
            pltpu.VMEM((ITERS - 1, 2, 4, 128), f32),
            pltpu.VMEM((ITERS - 1, 2, 7, 4, 128), f32),
            pltpu.VMEM((4, 4, 128), f32),
            pltpu.VMEM((4, 4, 128), f32),
            pltpu.VMEM((4, 2, 128), f32),
            pltpu.VMEM((32, 2, 128), f32),
            dma((4,)),
            dma((TILES,)),
            dma((TILES,)),
            dma((CHUNKS,)),
            dma((1,)),
            dma((1,)),
            dma((6,)),
            dma((ITERS, 2)),
            dma((ITERS, 2)),
            dma((ITERS - 1, 2)),
            dma((ITERS - 1, 2)),
            dma((1,)),
            dma((1,)),
            dma((1,)),
            dma((1,)),
        ],
        compiler_params=pltpu.CompilerParams(collective_id=0, has_side_effects=True, vmem_limit_bytes=VMEM_LIMIT),
    )(*[pltpu.with_memory_space_constraint(v, pltpu.HBM) for v in (source_points, target_points, source_mass.reshape(16, 128), target_mass.reshape(8, 128))])
    return f_scaled.reshape(2048) * (1.0 / ALPHA), g_scaled.reshape(1024) * (1.0 / ALPHA)


def solution(mesh):
    placed = (P(("src", "tgt"), None), P(("tgt", "src"), None), P("src"), P("tgt"))
    return jax.shard_map(
        local, mesh=mesh, in_specs=placed, out_specs=(P("src"), P("tgt")), check_vma=False
    )
```

```python
import math

import jax
import jax.numpy as jnp
from jax import lax
from jax.experimental import pallas as pl
from jax.experimental.pallas import tpu as pltpu
from jax.sharding import PartitionSpec as P

MESH = pl.DeviceIdType.MESH

ITERS = 3
EPS = 0.05
ALPHA = 1.0 / (EPS * math.log(2.0))
INV_LN2 = 1.0 / math.log(2.0)

TILES = 16
CHUNKS = 8
LINE = (4, 3, 5, 2, 6, 1, 7)
ORDER = (2, 6, 3, 5, 1, 7)
SETS = ((0, 1, 7, 2, 6), (3, 5, 4))
PLANE = sorted(
    ((dy, dx, dc) for dy in range(4) for dx in range(4) for dc in range(2) if dy or dx or dc),
    key=lambda p: -min(p[0], 4 - p[0]) - min(p[1], 4 - p[1]),
)
SHEET = sorted(
    ((dy, dz) for dy in range(4) for dz in range(8) if dy or dz), key=lambda p: -min(p[0], 4 - p[0]) - min(p[1], 8 - p[1])
)
CHIPS = [p for p in PLANE if p[2] == 0]
VMEM_LIMIT = 24 * 2**20


def log2(value):
    return jnp.log(value) * INV_LN2


def place(z, y, x, c):
    return {"src": (z // 4) * 4 + y, "tgt": (z % 4) * 8 + x * 2 + c}


def chunk_of(z):
    return (z % 4) * 2 + z // 4


def row_norm(points):
    values = points.astype(jnp.float32)
    square = values * values
    high = square.astype(jnp.bfloat16)
    low = (square - high.astype(jnp.float32)).astype(jnp.bfloat16)
    ones = jnp.ones((8, 128), jnp.bfloat16)
    dims = (((1,), (1,)), ((), ()))
    total = lax.dot_general(ones, high, dims, preferred_element_type=jnp.float32) + lax.dot_general(
        ones, low, dims, preferred_element_type=jnp.float32
    )
    return (0.5 * ALPHA) * total[0:1, :]


def to_column(row):
    return jnp.transpose(jnp.broadcast_to(row, (128, 128)))


def tree(op, values):
    values = list(values)
    while len(values) > 1:
        values = [op(*values[i : i + 2]) if i + 1 < len(values) else values[i] for i in range(0, len(values), 2)]
    return values[0]


def stats(pieces):
    peak = tree(jnp.maximum, pieces)
    return peak, tree(jnp.add, [jnp.exp2(piece - peak) for piece in pieces])


def join(first, second):
    peak = jnp.maximum(first[0], second[0])
    return peak, first[1] * jnp.exp2(first[0] - peak) + second[1] * jnp.exp2(second[0] - peak)


def merge(parts, own):
    top = jnp.maximum(jnp.max(parts, axis=0), own)
    return top + log2(jnp.sum(jnp.exp2(parts - top[None]), axis=0) + jnp.exp2(own - top))


def kernel(
    xs, ys, am, bm, out,
    X, Y, ST, CB, GM, GT, PM, PT, amv, bmv, aux_t, aux_s, logs_a, norm_x, r_rows,
    part_f, recv_f, part_g, recv_g, f_part, f_all, part_e, recv_e,
    local_sem, x_recv, fwd_recv, y_recv, at_recv, as_recv, send_sem,
    f_send, f_recv, g_send, g_recv, o_send, o_recv, e_send, e_recv,
):
    s = lax.axis_index("src")
    t = lax.axis_index("tgt")
    z = (s // 4) * 4 + t // 8
    y = s % 4
    x = (t // 2) % 4
    c = t % 2
    zl = z % 4
    tile = y * 4 + x
    q = chunk_of(z)

    z_at = [(z + p) % 8 for p in range(8)]
    src_z = [there // 4 * 4 for there in z_at]
    tgt_z = [there % 4 * 8 for there in z_at]
    zl_at = [there % 4 for there in z_at]
    y_at = [(y + p) % 4 for p in range(4)]
    x_at = [(x + p) % 4 for p in range(4)]
    tgt_x = [(x + p) % 4 * 2 for p in range(4)]
    tgt_c = [c, 1 - c]
    tgt_xc = [[tgt_z[0] + tgt_x[p] + tgt_c[r] for r in range(2)] for p in range(4)]
    src_y = [src_z[0] + y_at[p] for p in range(4)]
    tgt_own = tgt_x[0] + c

    def line(p):
        return {"src": src_z[p] + y, "tgt": tgt_z[p] + tgt_own}

    def plane(p):
        return {"src": src_y[p[0]], "tgt": tgt_xc[p[1]][p[2]]}

    sibling = plane((0, 0, 1))

    copies = [
        pltpu.make_async_copy(ys, Y.at[q], local_sem.at[0]),
        pltpu.make_async_copy(xs, X.at[tile, pl.ds(c * 64, 64)], local_sem.at[1]),
        pltpu.make_async_copy(bm, bmv, local_sem.at[2]),
        pltpu.make_async_copy(am, amv, local_sem.at[3]),
    ]
    for copy in copies:
        copy.start()

    barrier = pltpu.get_barrier_semaphore()

    for p in LINE:
        pl.semaphore_signal(barrier, inc=1, device_id=line(p), device_id_type=MESH)
    for p in PLANE:
        pl.semaphore_signal(barrier, inc=1, device_id=plane(p), device_id_type=MESH)

    for copy in copies:
        copy.wait()
    norm = row_norm(Y[q])
    aux_t[q, 0:1, :] = log2(bmv[pl.ds(s, 1), :]) - norm
    aux_t[q, 1:2, :] = norm
    aux_s[tile] = log2(amv[pl.ds(t // 2, 1), :])

    pl.semaphore_wait(barrier, 7 + 31)

    def remote(src, dst, send, recv, device):
        pltpu.make_async_remote_copy(
            src_ref=src, dst_ref=dst, send_sem=send, recv_sem=recv, device_id=device, device_id_type=MESH
        ).start()

    def arrived(ref, sem):
        pltpu.make_async_copy(ref, ref, sem).wait()

    own = (tile, pl.ds(c * 64, 64))
    for p in LINE:
        remote(aux_t.at[q], aux_t.at[q], send_sem.at[0], at_recv.at[0], line(p))
    for p in ORDER:
        remote(Y.at[q], Y.at[q], send_sem.at[1], y_recv.at[q], line(p))
    for p in CHIPS:
        remote(X.at[own], X.at[own], send_sem.at[2], x_recv.at[tile], plane(p))
    remote(X.at[own], X.at[own], send_sem.at[4], fwd_recv.at[tile], sibling)
    for p in CHIPS:
        remote(aux_s.at[tile], aux_s.at[tile], send_sem.at[3], as_recv.at[0], plane(p))

    def row_of(n):
        return (y + (n + 1) // 2 * (2 * (n % 2) - 1) + 4) % 4

    def forward(n):
        dy = (0, 1, 3, 2)[n]
        for dx in (0, 1, 3, 2):
            if (dy, dx) != (0, 0):
                there = y_at[dy] * 4 + x_at[dx]
                block = (there, pl.ds(c * 64, 64))
                arrived(X.at[block], x_recv.at[there])
                remote(X.at[block], X.at[block], send_sem.at[4], fwd_recv.at[there], sibling)

    def send_f(step, half):
        for i, p in enumerate(PLANE):
            remote(
                part_f.at[step, half], recv_f.at[step, half, i], f_send.at[step, half], f_recv.at[step, half], plane(p)
            )

    def finish_sources(step, half):
        peaks = GM[pl.ds(half * 8, 8)]
        top = jnp.max(peaks, axis=1)
        total = jnp.sum(GT[pl.ds(half * 8, 8)] * jnp.exp2(peaks - top[:, None, :]), axis=1)
        part_f[step, half] = top + log2(total)
        send_f(step, half)

    def scores(first, count, chunks, add):
        rows = jnp.concatenate([Y[k] for k in chunks], axis=0)
        tiles = X[pl.ds(first, count)].reshape(count * 128, 128)
        product = lax.dot_general(rows, tiles, (((1,), (1,)), ((), ())), preferred_element_type=jnp.float32)
        for m in range(count):
            found = []
            for u, k in enumerate(chunks):
                pieces = []
                for j in range(16):
                    piece = ALPHA * product[(u * 16 + j) * 8 : (u * 16 + j + 1) * 8, m * 128 : (m + 1) * 128]
                    ST[k, first + m, j * 8 : j * 8 + 8, :] = piece
                    pieces.append(piece + CB[k, j * 8 : j * 8 + 8, :])
                found.append(stats(pieces))
            if add:
                found.append((GM[first + m], GT[first + m]))
            GM[first + m], GT[first + m] = tree(join, found)

    def chunks_at(distances):
        return [chunk_of(z_at[p]) for p in distances]

    for n in range(3):
        forward(n)
        if n == 0:
            for p, rows in ((2, pl.ds(0, 64)), (6, pl.ds(64, 64))):
                k = chunk_of(z_at[p])
                arrived(Y.at[k], y_recv.at[k])
                remote(Y.at[k, rows], Y.at[k, rows], send_sem.at[5], y_recv.at[k], line(8 - p))
    arrived(aux_t.at[pl.ds(0, 7)], at_recv.at[0])
    for k in range(CHUNKS):
        CB[k] = to_column(aux_t[k, 0:1, :])
    forward(3)
    for k in chunks_at(p for p in SETS[0] if p not in (0, 2, 6)):
        arrived(Y.at[k], y_recv.at[k])

    def early(n, carry):
        row = row_of(n)
        for x_there in range(4):
            there = row * 4 + x_there
            arrived(X.at[there, pl.ds((1 - c) * 64, 64)], fwd_recv.at[there])
        scores(row * 4, 4, chunks_at(SETS[0]), False)
        return carry

    lax.fori_loop(0, 4, early, 0)
    for k in chunks_at(p for p in SETS[1] if p not in (0, 2, 6)):
        arrived(Y.at[k], y_recv.at[k])

    def late(half, carry):
        scores(half * 8, 8, chunks_at(SETS[1]), True)
        finish_sources(0, half)
        return carry

    lax.fori_loop(0, 2, late, 0)

    arrived(aux_s.at[pl.ds(0, 15)], as_recv.at[0])
    for half in range(2):
        logs_a[half] = jnp.concatenate([aux_s[half * 8 + m] for m in range(8)], axis=0)

    def norms(m, carry):
        norm_x[m] = row_norm(X[m])
        return carry

    lax.fori_loop(0, TILES, norms, 0)

    def merged_f(step, half):
        arrived(recv_f.at[step, half], f_recv.at[step, half])
        total = merge(recv_f[step, half], part_f[step, half])
        r_rows[half] = logs_a[half] - total
        return total

    def target_pieces(k, j, half):
        return [
            ST[k, half * 8 + m, j * 8 : j * 8 + 8, :] + r_rows[half, m : m + 1, :] for m in range(8)
        ]

    def target_first():
        def chunk(i, carry):
            for k in (i * 2, i * 2 + 1):
                for j in range(16):
                    rows = slice(j * 8, j * 8 + 8)
                    PM[k, rows, :], PT[k, rows, :] = stats(target_pieces(k, j, 0))
            return carry

        lax.fori_loop(0, CHUNKS // 2, chunk, 0)

    def target_second(half):
        results = []
        for i in range(4):
            k = half * 4 + i
            values = []
            for j in range(16):
                rows = slice(j * 8, j * 8 + 8)
                found = join((PM[k, rows, :], PT[k, rows, :]), stats(target_pieces(k, j, 1)))
                values.append(found[0] + log2(found[1]))
            turned = jnp.transpose(jnp.concatenate(values, axis=0))
            top = jnp.max(turned, axis=0, keepdims=True)
            results.append(top + log2(jnp.sum(jnp.exp2(turned - top), axis=0, keepdims=True)))
        return results

    def merged_g(step, half):
        arrived(recv_g.at[step, half], g_recv.at[step, half])
        total = merge(recv_g[step, half], part_g[step, half])
        for i in range(4):
            k = half * 4 + i
            CB[k] = to_column(aux_t[k, 0:1, :] + aux_t[k, 1:2, :] - total[i : i + 1, :])

    def source_tiles(first, half):
        for u in range(4):
            m = first + u
            for k in range(half * 4, half * 4 + 4):
                found = stats(
                    [ST[k, m, j * 8 : j * 8 + 8, :] + CB[k, j * 8 : j * 8 + 8, :] for j in range(16)]
                )
                state = found if k == half * 4 else join(state, found)
            if half == 1:
                state = join((GM[m], GT[m]), state)
            GM[m], GT[m] = state

    last = ITERS - 1

    def iteration(step, carry):
        first = merged_f(step, 0)
        target_first()
        second = merged_f(step, 1)

        def target_half(half, carry):
            rows = target_second(half)

            @pl.when(step < last)
            def _():
                for i, row in enumerate(rows):
                    part_g[step, half, i : i + 1, :] = row
                for i, p in enumerate(LINE):
                    remote(
                        part_g.at[step, half], recv_g.at[step, half, i], g_send.at[step, half], g_recv.at[step, half], line(p)
                    )

            @pl.when(step == last)
            def _():
                for i, row in enumerate(rows):
                    part_e[half * 2 + i // 2, i % 2 : i % 2 + 1, :] = row - aux_t[half * 4 + i, 1:2, :]
                for dy, dz in SHEET:

                    @pl.when(zl_at[dz] // 2 == half)
                    def _():
                        remote(
                            part_e.at[zl_at[dz]], recv_e.at[y * 8 + z], e_send.at[0], e_recv.at[0],
                            {"src": src_z[dz] + y_at[dy], "tgt": tgt_z[dz] + tgt_own},
                        )


            return carry

        lax.fori_loop(0, 2, target_half, 0)

        @pl.when(step < last)
        def _():
            merged_g(step, 0)

            def first_tiles(i, carry):
                source_tiles(i * 4, 0)
                return carry

            lax.fori_loop(0, 4, first_tiles, 0)
            merged_g(step, 1)

            def source_half(half, carry):
                for i in range(2):
                    source_tiles(half * 8 + i * 4, 1)
                finish_sources(step + 1, half)
                return carry

            lax.fori_loop(0, 2, source_half, 0)

        @pl.when(step == last)
        def _():
            for half, total in enumerate((first, second)):
                for m in range(8):
                    there = half * 8 + m
                    f_part[there // 4, there % 4 : there % 4 + 1, :] = norm_x[there] - total[m : m + 1, :]

        return carry

    lax.fori_loop(0, ITERS, iteration, 0)

    f_all[zl] = f_part[y]
    for p in range(1, 4):
        device = {"src": src_y[0], "tgt": (zl + p) % 4 * 8 + tgt_own}
        remote(f_part.at[y], f_all.at[zl], o_send.at[0], o_recv.at[0], device)
    recv_e[y * 8 + z] = part_e[zl]

    arrived(f_all.at[pl.ds(0, 3)], o_recv.at[0])
    for there in range(4):
        out[there * 4 : there * 4 + 4, :] = f_all[there]
    arrived(aux_t.at[pl.ds(0, 7)], send_sem.at[0])
    arrived(Y.at[pl.ds(0, 6)], send_sem.at[1])
    arrived(Y.at[0], send_sem.at[5])
    arrived(X.at[pl.ds(0, 15), pl.ds(0, 64)], send_sem.at[2])
    arrived(aux_s.at[pl.ds(0, 15)], send_sem.at[3])
    arrived(X.at[pl.ds(0, 16), pl.ds(0, 64)], send_sem.at[4])
    for step in range(ITERS):
        for half in range(2):
            arrived(recv_f.at[step, half], f_send.at[step, half])
            if step < last:
                arrived(recv_g.at[step, half], g_send.at[step, half])
    arrived(f_all.at[pl.ds(0, 3)], o_send.at[0])
    arrived(recv_e.at[pl.ds(0, 31)], e_send.at[0])

    arrived(recv_e.at[pl.ds(0, 31)], e_recv.at[0])
    for there in range(4):
        parts = recv_e[there * 8 : there * 8 + 8]
        total = merge(parts[1:], parts[0])
        for half in range(2):
            out[16 + half * 4 + there : 17 + half * 4 + there, :] = -total[half : half + 1, :]


def local(source_points, target_points, source_mass, target_mass):
    f32, bf16 = jnp.float32, jnp.bfloat16
    dma = pltpu.SemaphoreType.DMA
    scaled = pl.pallas_call(
        kernel,
        out_shape=jax.ShapeDtypeStruct((24, 128), f32),
        in_specs=[pl.BlockSpec(memory_space=pl.ANY)] * 4,
        out_specs=pl.BlockSpec(memory_space=pltpu.VMEM),
        scratch_shapes=[
            pltpu.VMEM((TILES, 128, 128), bf16),
            pltpu.VMEM((CHUNKS, 128, 128), bf16),
            pltpu.VMEM((CHUNKS, TILES, 128, 128), f32),
            pltpu.VMEM((CHUNKS, 128, 128), f32),
            pltpu.VMEM((TILES, 8, 128), f32),
            pltpu.VMEM((TILES, 8, 128), f32),
            pltpu.VMEM((CHUNKS, 128, 128), f32),
            pltpu.VMEM((CHUNKS, 128, 128), f32),
            pltpu.VMEM((16, 128), f32),
            pltpu.VMEM((8, 128), f32),
            pltpu.VMEM((CHUNKS, 2, 128), f32),
            pltpu.VMEM((TILES, 1, 128), f32),
            pltpu.VMEM((2, 8, 128), f32),
            pltpu.VMEM((TILES, 1, 128), f32),
            pltpu.VMEM((2, 8, 128), f32),
            pltpu.VMEM((ITERS, 2, 8, 128), f32),
            pltpu.VMEM((ITERS, 2, 31, 8, 128), f32),
            pltpu.VMEM((ITERS - 1, 2, 4, 128), f32),
            pltpu.VMEM((ITERS - 1, 2, 7, 4, 128), f32),
            pltpu.VMEM((4, 4, 128), f32),
            pltpu.VMEM((4, 4, 128), f32),
            pltpu.VMEM((4, 2, 128), f32),
            pltpu.VMEM((32, 2, 128), f32),
            dma((4,)),
            dma((TILES,)),
            dma((TILES,)),
            dma((CHUNKS,)),
            dma((1,)),
            dma((1,)),
            dma((6,)),
            dma((ITERS, 2)),
            dma((ITERS, 2)),
            dma((ITERS - 1, 2)),
            dma((ITERS - 1, 2)),
            dma((1,)),
            dma((1,)),
            dma((1,)),
            dma((1,)),
        ],
        compiler_params=pltpu.CompilerParams(collective_id=0, has_side_effects=True, vmem_limit_bytes=VMEM_LIMIT),
    )(*[pltpu.with_memory_space_constraint(v, pltpu.HBM) for v in (source_points, target_points, source_mass.reshape(16, 128), target_mass.reshape(8, 128))])
    return scaled[:16].reshape(2048) * (1.0 / ALPHA), scaled[16:].reshape(1024) * (1.0 / ALPHA)


def solution(mesh):
    placed = (P(("src", "tgt"), None), P(("tgt", "src"), None), P("src"), P("tgt"))
    return jax.shard_map(
        local, mesh=mesh, in_specs=placed, out_specs=(P("src"), P("tgt")), check_vma=False
    )
```

```python
import math

import jax
import jax.numpy as jnp
from jax import lax
from jax.experimental import pallas as pl
from jax.experimental.pallas import tpu as pltpu
from jax.sharding import PartitionSpec as P

MESH = pl.DeviceIdType.MESH

ITERS = 3
EPS = 0.05
ALPHA = 1.0 / (EPS * math.log(2.0))
INV_LN2 = 1.0 / math.log(2.0)

TILES = 16
CHUNKS = 8
LINE = (4, 3, 5, 2, 6, 1, 7)
ORDER = (2, 6, 1, 7)
SETS = ((0, 1, 7, 2, 6), (3, 5, 4))
PLANE = sorted(
    ((dy, dx, dc) for dy in range(4) for dx in range(4) for dc in range(2) if dy or dx or dc),
    key=lambda p: -min(p[0], 4 - p[0]) - min(p[1], 4 - p[1]),
)
SHEET = sorted(
    ((dy, dz) for dy in range(4) for dz in range(8) if dy or dz), key=lambda p: -min(p[0], 4 - p[0]) - min(p[1], 8 - p[1])
)
CHIPS = [p for p in PLANE if p[2] == 0]
VMEM_LIMIT = 24 * 2**20


def log2(value):
    return jnp.log(value) * INV_LN2


def place(z, y, x, c):
    return {"src": (z // 4) * 4 + y, "tgt": (z % 4) * 8 + x * 2 + c}


def chunk_of(z):
    return (z % 4) * 2 + z // 4


def row_norm(points):
    values = points.astype(jnp.float32)
    square = values * values
    high = square.astype(jnp.bfloat16)
    low = (square - high.astype(jnp.float32)).astype(jnp.bfloat16)
    ones = jnp.ones((8, 128), jnp.bfloat16)
    dims = (((1,), (1,)), ((), ()))
    total = lax.dot_general(ones, high, dims, preferred_element_type=jnp.float32) + lax.dot_general(
        ones, low, dims, preferred_element_type=jnp.float32
    )
    return (0.5 * ALPHA) * total[0:1, :]


def to_column(row):
    return jnp.transpose(jnp.broadcast_to(row, (128, 128)))


def tree(op, values):
    values = list(values)
    while len(values) > 1:
        values = [op(*values[i : i + 2]) if i + 1 < len(values) else values[i] for i in range(0, len(values), 2)]
    return values[0]


def stats(pieces):
    peak = tree(jnp.maximum, pieces)
    return peak, tree(jnp.add, [jnp.exp2(piece - peak) for piece in pieces])


def join(first, second):
    peak = jnp.maximum(first[0], second[0])
    return peak, first[1] * jnp.exp2(first[0] - peak) + second[1] * jnp.exp2(second[0] - peak)


def merge(parts, own):
    top = jnp.maximum(jnp.max(parts, axis=0), own)
    return top + log2(jnp.sum(jnp.exp2(parts - top[None]), axis=0) + jnp.exp2(own - top))


def kernel(
    xs, ys, am, bm, out,
    X, Y, ST, CB, GM, GT, PM, PT, amv, bmv, aux_t, aux_s, logs_a, norm_x, r_rows,
    part_f, recv_f, part_g, recv_g, f_part, f_all, part_e, recv_e,
    local_sem, x_recv, fwd_recv, y_recv, at_recv, as_recv, send_sem,
    f_send, f_recv, g_send, g_recv, o_send, o_recv, e_send, e_recv,
):
    s = lax.axis_index("src")
    t = lax.axis_index("tgt")
    z = (s // 4) * 4 + t // 8
    y = s % 4
    x = (t // 2) % 4
    c = t % 2
    zl = z % 4
    tile = y * 4 + x
    q = chunk_of(z)

    z_at = [(z + p) % 8 for p in range(8)]
    src_z = [there // 4 * 4 for there in z_at]
    tgt_z = [there % 4 * 8 for there in z_at]
    zl_at = [there % 4 for there in z_at]
    y_at = [(y + p) % 4 for p in range(4)]
    x_at = [(x + p) % 4 for p in range(4)]
    tgt_x = [(x + p) % 4 * 2 for p in range(4)]
    tgt_c = [c, 1 - c]
    tgt_xc = [[tgt_z[0] + tgt_x[p] + tgt_c[r] for r in range(2)] for p in range(4)]
    src_y = [src_z[0] + y_at[p] for p in range(4)]
    tgt_own = tgt_x[0] + c

    def line(p):
        return {"src": src_z[p] + y, "tgt": tgt_z[p] + tgt_own}

    def plane(p):
        return {"src": src_y[p[0]], "tgt": tgt_xc[p[1]][p[2]]}

    sibling = plane((0, 0, 1))

    copies = [
        pltpu.make_async_copy(ys, Y.at[q], local_sem.at[0]),
        pltpu.make_async_copy(xs, X.at[tile, pl.ds(c * 64, 64)], local_sem.at[1]),
        pltpu.make_async_copy(bm, bmv, local_sem.at[2]),
        pltpu.make_async_copy(am, amv, local_sem.at[3]),
    ]
    for copy in copies:
        copy.start()

    barrier = pltpu.get_barrier_semaphore()

    for p in LINE:
        pl.semaphore_signal(barrier, inc=1, device_id=line(p), device_id_type=MESH)
    for p in PLANE:
        pl.semaphore_signal(barrier, inc=1, device_id=plane(p), device_id_type=MESH)

    for copy in copies:
        copy.wait()
    norm = row_norm(Y[q])
    aux_t[q, 0:1, :] = log2(bmv[pl.ds(s, 1), :]) - norm
    aux_t[q, 1:2, :] = norm
    aux_s[tile] = log2(amv[pl.ds(t // 2, 1), :])

    pl.semaphore_wait(barrier, 7 + 31)

    def remote(src, dst, send, recv, device):
        pltpu.make_async_remote_copy(
            src_ref=src, dst_ref=dst, send_sem=send, recv_sem=recv, device_id=device, device_id_type=MESH
        ).start()

    def arrived(ref, sem):
        pltpu.make_async_copy(ref, ref, sem).wait()

    own = (tile, pl.ds(c * 64, 64))
    for p in LINE:
        remote(aux_t.at[q], aux_t.at[q], send_sem.at[0], at_recv.at[0], line(p))
    for p in ORDER:
        remote(Y.at[q], Y.at[q], send_sem.at[1], y_recv.at[q], line(p))
    for p in CHIPS:
        remote(X.at[own], X.at[own], send_sem.at[2], x_recv.at[tile], plane(p))
    remote(X.at[own], X.at[own], send_sem.at[4], fwd_recv.at[tile], sibling)
    for p in CHIPS:
        remote(aux_s.at[tile], aux_s.at[tile], send_sem.at[3], as_recv.at[0], plane(p))

    def row_of(n):
        return (y + (n + 1) // 2 * (2 * (n % 2) - 1) + 4) % 4

    def forward(n):
        dy = (0, 1, 3, 2)[n]
        for dx in (0, 1, 3, 2):
            if (dy, dx) != (0, 0):
                there = y_at[dy] * 4 + x_at[dx]
                block = (there, pl.ds(c * 64, 64))
                arrived(X.at[block], x_recv.at[there])
                remote(X.at[block], X.at[block], send_sem.at[4], fwd_recv.at[there], sibling)

    def send_f(step, half):
        for i, p in enumerate(PLANE):
            remote(
                part_f.at[step, half], recv_f.at[step, half, i], f_send.at[step, half], f_recv.at[step, half], plane(p)
            )

    def finish_sources(step, half):
        peaks = GM[pl.ds(half * 8, 8)]
        top = jnp.max(peaks, axis=1)
        total = jnp.sum(GT[pl.ds(half * 8, 8)] * jnp.exp2(peaks - top[:, None, :]), axis=1)
        part_f[step, half] = top + log2(total)
        send_f(step, half)

    def scores(first, count, chunks, add):
        rows = jnp.concatenate([Y[k] for k in chunks], axis=0)
        tiles = X[pl.ds(first, count)].reshape(count * 128, 128)
        product = lax.dot_general(rows, tiles, (((1,), (1,)), ((), ())), preferred_element_type=jnp.float32)
        for m in range(count):
            found = []
            for u, k in enumerate(chunks):
                pieces = []
                for j in range(16):
                    piece = ALPHA * product[(u * 16 + j) * 8 : (u * 16 + j + 1) * 8, m * 128 : (m + 1) * 128]
                    ST[k, first + m, j * 8 : j * 8 + 8, :] = piece
                    pieces.append(piece + CB[k, j * 8 : j * 8 + 8, :])
                found.append(stats(pieces))
            if add:
                found.append((GM[first + m], GT[first + m]))
            GM[first + m], GT[first + m] = tree(join, found)

    def chunks_at(distances):
        return [chunk_of(z_at[p]) for p in distances]

    for p, rows in ((2, pl.ds(0, 64)), (6, pl.ds(64, 64))):
        k = chunk_of(z_at[p])
        arrived(Y.at[k], y_recv.at[k])
        remote(Y.at[k], Y.at[k], send_sem.at[5], y_recv.at[k], line(7 if p == 2 else 1))
        remote(Y.at[k, rows], Y.at[k, rows], send_sem.at[5], y_recv.at[k], line(8 - p))
    for n in range(3):
        forward(n)
    arrived(aux_t.at[pl.ds(0, 7)], at_recv.at[0])
    for k in range(CHUNKS):
        CB[k] = to_column(aux_t[k, 0:1, :])
    forward(3)
    for k in chunks_at(p for p in SETS[0] if p not in (0, 2, 6)):
        arrived(Y.at[k], y_recv.at[k])

    def early(n, carry):
        row = row_of(n)
        for x_there in range(4):
            there = row * 4 + x_there
            arrived(X.at[there, pl.ds((1 - c) * 64, 64)], fwd_recv.at[there])
        scores(row * 4, 4, chunks_at(SETS[0]), False)
        return carry

    lax.fori_loop(0, 4, early, 0)
    for k in chunks_at(p for p in SETS[1] if p not in (0, 2, 6)):
        arrived(Y.at[k], y_recv.at[k])

    def late(half, carry):
        scores(half * 8, 8, chunks_at(SETS[1]), True)
        finish_sources(0, half)
        return carry

    lax.fori_loop(0, 2, late, 0)

    arrived(aux_s.at[pl.ds(0, 15)], as_recv.at[0])
    for half in range(2):
        logs_a[half] = jnp.concatenate([aux_s[half * 8 + m] for m in range(8)], axis=0)

    def norms(m, carry):
        norm_x[m] = row_norm(X[m])
        return carry

    lax.fori_loop(0, TILES, norms, 0)

    def merged_f(step, half):
        arrived(recv_f.at[step, half], f_recv.at[step, half])
        total = merge(recv_f[step, half], part_f[step, half])
        r_rows[half] = logs_a[half] - total
        return total

    def target_pieces(k, j, half):
        return [
            ST[k, half * 8 + m, j * 8 : j * 8 + 8, :] + r_rows[half, m : m + 1, :] for m in range(8)
        ]

    def target_first():
        def chunk(i, carry):
            for k in (i * 2, i * 2 + 1):
                for j in range(16):
                    rows = slice(j * 8, j * 8 + 8)
                    PM[k, rows, :], PT[k, rows, :] = stats(target_pieces(k, j, 0))
            return carry

        lax.fori_loop(0, CHUNKS // 2, chunk, 0)

    def target_second(half):
        results = []
        for i in range(4):
            k = half * 4 + i
            values = []
            for j in range(16):
                rows = slice(j * 8, j * 8 + 8)
                found = join((PM[k, rows, :], PT[k, rows, :]), stats(target_pieces(k, j, 1)))
                values.append(found[0] + log2(found[1]))
            turned = jnp.transpose(jnp.concatenate(values, axis=0))
            top = jnp.max(turned, axis=0, keepdims=True)
            results.append(top + log2(jnp.sum(jnp.exp2(turned - top), axis=0, keepdims=True)))
        return results

    def merged_g(step, half):
        arrived(recv_g.at[step, half], g_recv.at[step, half])
        total = merge(recv_g[step, half], part_g[step, half])
        for i in range(4):
            k = half * 4 + i
            CB[k] = to_column(aux_t[k, 0:1, :] + aux_t[k, 1:2, :] - total[i : i + 1, :])

    def source_tiles(first, half):
        for u in range(4):
            m = first + u
            for k in range(half * 4, half * 4 + 4):
                found = stats(
                    [ST[k, m, j * 8 : j * 8 + 8, :] + CB[k, j * 8 : j * 8 + 8, :] for j in range(16)]
                )
                state = found if k == half * 4 else join(state, found)
            if half == 1:
                state = join((GM[m], GT[m]), state)
            GM[m], GT[m] = state

    last = ITERS - 1

    def iteration(step, carry):
        first = merged_f(step, 0)
        target_first()
        second = merged_f(step, 1)

        def target_half(half, carry):
            rows = target_second(half)

            @pl.when(step < last)
            def _():
                for i, row in enumerate(rows):
                    part_g[step, half, i : i + 1, :] = row
                for i, p in enumerate(LINE):
                    remote(
                        part_g.at[step, half], recv_g.at[step, half, i], g_send.at[step, half], g_recv.at[step, half], line(p)
                    )

            @pl.when(step == last)
            def _():
                for i, row in enumerate(rows):
                    part_e[half * 2 + i // 2, i % 2 : i % 2 + 1, :] = row - aux_t[half * 4 + i, 1:2, :]
                for dy, dz in SHEET:

                    @pl.when(zl_at[dz] // 2 == half)
                    def _():
                        remote(
                            part_e.at[zl_at[dz]], recv_e.at[y * 8 + z], e_send.at[0], e_recv.at[0],
                            {"src": src_z[dz] + y_at[dy], "tgt": tgt_z[dz] + tgt_own},
                        )


            return carry

        lax.fori_loop(0, 2, target_half, 0)

        @pl.when(step < last)
        def _():
            merged_g(step, 0)

            def first_tiles(i, carry):
                source_tiles(i * 4, 0)
                return carry

            lax.fori_loop(0, 4, first_tiles, 0)
            merged_g(step, 1)

            def source_half(half, carry):
                for i in range(2):
                    source_tiles(half * 8 + i * 4, 1)
                finish_sources(step + 1, half)
                return carry

            lax.fori_loop(0, 2, source_half, 0)

        @pl.when(step == last)
        def _():
            for half, total in enumerate((first, second)):
                for m in range(8):
                    there = half * 8 + m
                    f_part[there // 4, there % 4 : there % 4 + 1, :] = norm_x[there] - total[m : m + 1, :]

        return carry

    lax.fori_loop(0, ITERS, iteration, 0)

    f_all[zl] = f_part[y]
    for p in range(1, 4):
        device = {"src": src_y[0], "tgt": (zl + p) % 4 * 8 + tgt_own}
        remote(f_part.at[y], f_all.at[zl], o_send.at[0], o_recv.at[0], device)
    recv_e[y * 8 + z] = part_e[zl]

    arrived(f_all.at[pl.ds(0, 3)], o_recv.at[0])
    for there in range(4):
        out[there * 4 : there * 4 + 4, :] = f_all[there]
    arrived(aux_t.at[pl.ds(0, 7)], send_sem.at[0])
    arrived(Y.at[pl.ds(0, 4)], send_sem.at[1])
    arrived(Y.at[pl.ds(0, 3)], send_sem.at[5])
    arrived(X.at[pl.ds(0, 15), pl.ds(0, 64)], send_sem.at[2])
    arrived(aux_s.at[pl.ds(0, 15)], send_sem.at[3])
    arrived(X.at[pl.ds(0, 16), pl.ds(0, 64)], send_sem.at[4])
    for step in range(ITERS):
        for half in range(2):
            arrived(recv_f.at[step, half], f_send.at[step, half])
            if step < last:
                arrived(recv_g.at[step, half], g_send.at[step, half])
    arrived(f_all.at[pl.ds(0, 3)], o_send.at[0])
    arrived(recv_e.at[pl.ds(0, 31)], e_send.at[0])

    arrived(recv_e.at[pl.ds(0, 31)], e_recv.at[0])
    for there in range(4):
        parts = recv_e[there * 8 : there * 8 + 8]
        total = merge(parts[1:], parts[0])
        for half in range(2):
            out[16 + half * 4 + there : 17 + half * 4 + there, :] = -total[half : half + 1, :]


def local(source_points, target_points, source_mass, target_mass):
    f32, bf16 = jnp.float32, jnp.bfloat16
    dma = pltpu.SemaphoreType.DMA
    scaled = pl.pallas_call(
        kernel,
        out_shape=jax.ShapeDtypeStruct((24, 128), f32),
        in_specs=[pl.BlockSpec(memory_space=pl.ANY)] * 4,
        out_specs=pl.BlockSpec(memory_space=pltpu.VMEM),
        scratch_shapes=[
            pltpu.VMEM((TILES, 128, 128), bf16),
            pltpu.VMEM((CHUNKS, 128, 128), bf16),
            pltpu.VMEM((CHUNKS, TILES, 128, 128), f32),
            pltpu.VMEM((CHUNKS, 128, 128), f32),
            pltpu.VMEM((TILES, 8, 128), f32),
            pltpu.VMEM((TILES, 8, 128), f32),
            pltpu.VMEM((CHUNKS, 128, 128), f32),
            pltpu.VMEM((CHUNKS, 128, 128), f32),
            pltpu.VMEM((16, 128), f32),
            pltpu.VMEM((8, 128), f32),
            pltpu.VMEM((CHUNKS, 2, 128), f32),
            pltpu.VMEM((TILES, 1, 128), f32),
            pltpu.VMEM((2, 8, 128), f32),
            pltpu.VMEM((TILES, 1, 128), f32),
            pltpu.VMEM((2, 8, 128), f32),
            pltpu.VMEM((ITERS, 2, 8, 128), f32),
            pltpu.VMEM((ITERS, 2, 31, 8, 128), f32),
            pltpu.VMEM((ITERS - 1, 2, 4, 128), f32),
            pltpu.VMEM((ITERS - 1, 2, 7, 4, 128), f32),
            pltpu.VMEM((4, 4, 128), f32),
            pltpu.VMEM((4, 4, 128), f32),
            pltpu.VMEM((4, 2, 128), f32),
            pltpu.VMEM((32, 2, 128), f32),
            dma((4,)),
            dma((TILES,)),
            dma((TILES,)),
            dma((CHUNKS,)),
            dma((1,)),
            dma((1,)),
            dma((6,)),
            dma((ITERS, 2)),
            dma((ITERS, 2)),
            dma((ITERS - 1, 2)),
            dma((ITERS - 1, 2)),
            dma((1,)),
            dma((1,)),
            dma((1,)),
            dma((1,)),
        ],
        compiler_params=pltpu.CompilerParams(collective_id=0, has_side_effects=True, vmem_limit_bytes=VMEM_LIMIT),
    )(*[pltpu.with_memory_space_constraint(v, pltpu.HBM) for v in (source_points, target_points, source_mass.reshape(16, 128), target_mass.reshape(8, 128))])
    return scaled[:16].reshape(2048) * (1.0 / ALPHA), scaled[16:].reshape(1024) * (1.0 / ALPHA)


def solution(mesh):
    placed = (P(("src", "tgt"), None), P(("tgt", "src"), None), P("src"), P("tgt"))
    return jax.shard_map(
        local, mesh=mesh, in_specs=placed, out_specs=(P("src"), P("tgt")), check_vma=False
    )
```
